32 devices in a mesh: seq: 8 (over y, x, core), dp: 4 (over z).
Axes of the slice: x: 2, y: 2, z: 4, core: 2. Of those that a mesh axis runs over, the one named last changes fastest.
Arguments:
- queries: bfloat16 [4, 8, 1024, 1024], P('dp', 'seq'), may hold values from -6 to 6
- keys: bfloat16 [4, 8, 1024, 1024], P('dp', 'seq'), may hold values from -6 to 6
- values: bfloat16 [4, 8, 1024, 1024], P('dp', 'seq'), may hold values from -6 to 6
- out_weight: bfloat16 [1024, 2048], P(('seq', 'dp')), may hold values from -0.1875 to 0.1875
- cotangent: bfloat16 [4, 8, 1024, 2048], P('dp', 'seq'), may hold values from -6 to 6
Outputs:
- layer_out: bfloat16 [4, 8, 1024, 2048], P('dp', 'seq')
- query_grad: bfloat16 [4, 8, 1024, 1024], P('dp', 'seq')
- key_grad: bfloat16 [4, 8, 1024, 1024], P('dp', 'seq')
- value_grad: bfloat16 [4, 8, 1024, 1024], P('dp', 'seq')
- weight_grad: float32 [1024, 2048], P(('seq', 'dp'))
The draws below stay inside these ranges and needn't reach their ends.
All inputs are finite; a program needn't handle non-finite values.
Results may differ from the reference program's by a relative error of at most 0.0071.
Values may be sent and summed in bfloat16 or wider, within the bound.
No kernel may reach another device: no remote copies, remote signals or barrier semaphores. Data moves between devices by JAX's collectives and lax.ppermute only.
A program may use at most 128 MiB of HBM per device.

```python
import math
import jax
import jax.numpy as jnp
from jax import lax

D = 2048
ROW_HEADS = 4
COL_HEADS = 4
DH = 128
STRIDE = 1024
ROWS = 8
SEQS = 4
ALL_TOKENS = 32768


def drawn_draw(key, salt):
    head_width = (ROW_HEADS + COL_HEADS) * DH
    noise = jax.random.truncated_normal(jax.random.fold_in(key, salt), -4.0, 4.0, (SEQS, ROWS, STRIDE, head_width), jnp.float32) * 1.4
    return noise


def draw_queries(key, part):
    return drawn_draw(key, 11).astype(jnp.bfloat16)


def draw_keys(key, part):
    return drawn_draw(key, 13).astype(jnp.bfloat16)


def level_of(own_key, extent, pieces, smallest, largest):
    factor_of = 1.0
    for position, blocks in pieces:
        steps = jax.random.uniform(jax.random.fold_in(jax.random.fold_in(own_key, 6), position), (blocks,), jnp.float32, smallest / len(pieces), largest / len(pieces))
        factor_of = factor_of * jnp.repeat(jnp.exp(steps), extent[position] // blocks).reshape((-1,) + (1,) * (len(extent) - 1 - position))
    return factor_of


def centred(own_key, dims, scale, most, cuts=(), dtype=jnp.bfloat16):
    result = jax.random.normal(own_key, dims, jnp.float32) * scale
    if len(cuts) > 0:
        result = level_of(own_key, dims, cuts, -0.22, 0.18) * result
    return jnp.clip(result, min=-most, max=most).astype(dtype)


def setup_inputs(seed: int = 0) -> dict:
    streams_of = jax.random.split(jax.random.key(seed), 6)
    queries = draw_queries(jax.random.fold_in(streams_of[5], 71), 0)
    keys = draw_keys(jax.random.fold_in(streams_of[5], 71), 0)
    values = centred(streams_of[2], (SEQS, ROWS, STRIDE, (ROW_HEADS + COL_HEADS) * DH), 1.0, 6.0, ((0, 4), (1, 8)))
    out_weight = centred(streams_of[3], ((ROW_HEADS + COL_HEADS) * DH, D), ((ROW_HEADS + COL_HEADS) * DH) ** -0.5, 0.1875, ((0, 32),))
    cotangent = centred(streams_of[4], (SEQS, ROWS, STRIDE, D), 1.0, 6.0, ((0, 4), (1, 8)))
    return dict(queries=queries, keys=keys, values=values, out_weight=out_weight, cotangent=cotangent)


def attend_sets(query_set, key_set, value_set, upstream_set):
    factor = 1.0 / math.sqrt(query_set.shape[-1])
    query_wide = query_set.astype(jnp.float32)
    key_wide = key_set.astype(jnp.float32)
    value_wide = value_set.astype(jnp.float32)
    upstream_wide = upstream_set.astype(jnp.float32)
    scores = jnp.einsum('...ld,...md->...lm', query_wide, key_wide) * factor
    length = scores.shape[-1]
    masked_out = lax.broadcasted_iota(jnp.int32, (length, length), 1) > lax.broadcasted_iota(jnp.int32, (length, length), 0)
    scores = jnp.where(masked_out, -jnp.inf, scores)
    peak_score = lax.optimization_barrier(jnp.max(scores, axis=-1, keepdims=True))
    raised = jnp.exp(scores - peak_score)
    shares = raised / lax.optimization_barrier(jnp.sum(raised, axis=-1, keepdims=True))
    shares_low = lax.optimization_barrier(shares.astype(jnp.bfloat16)).astype(jnp.float32)
    output = jnp.einsum('...lm,...md->...ld', shares_low, value_wide).astype(jnp.bfloat16)
    share_grad = jnp.einsum('...ld,...md->...lm', upstream_wide, value_wide)
    value_grad = jnp.einsum('...lm,...ld->...md', shares_low, upstream_wide).astype(jnp.bfloat16)
    row_total = lax.optimization_barrier(jnp.sum(shares * share_grad, axis=-1, keepdims=True))
    score_low = lax.optimization_barrier((shares * (share_grad - row_total)).astype(jnp.bfloat16)).astype(jnp.float32)
    query_grad = (jnp.einsum('...lm,...md->...ld', score_low, key_wide) * factor).astype(jnp.bfloat16)
    key_grad = (jnp.einsum('...lm,...ld->...md', score_low, query_wide) * factor).astype(jnp.bfloat16)
    return (output, query_grad, key_grad, value_grad)

def group_step(grouped):
    return attend_sets(grouped[0], grouped[1], grouped[2], grouped[3])

def reference(queries, keys, values, out_weight, cotangent):
    head_count = ROW_HEADS + COL_HEADS
    head_width = head_count * DH
    flat_cot = cotangent.reshape(-1, D)
    upstream = jnp.dot(flat_cot, out_weight.T, preferred_element_type=jnp.float32).astype(jnp.bfloat16)
    upstream = upstream.reshape(SEQS, ROWS, STRIDE, head_width)
    stacked = [member.reshape(SEQS, ROWS, STRIDE, head_count, DH) for member in (queries, keys, values, upstream)]
    row_parts = tuple((jnp.transpose(member[:, :, :, :ROW_HEADS], (0, 1, 3, 2, 4)).reshape(SEQS * ROWS, ROW_HEADS, STRIDE, DH) for member in stacked))
    row_results = lax.map(group_step, row_parts)
    row_back = [jnp.transpose(member.reshape(SEQS, ROWS, ROW_HEADS, STRIDE, DH), (0, 1, 3, 2, 4)) for member in row_results]
    col_parts = tuple((jnp.transpose(member[:, :, :, ROW_HEADS:], (0, 2, 3, 1, 4)) for member in stacked))
    col_results = lax.map(group_step, col_parts)
    col_back = [jnp.transpose(member, (0, 3, 1, 2, 4)) for member in col_results]
    joined = [jnp.concatenate([first_part, second_part], axis=3).reshape(SEQS, ROWS, STRIDE, head_width) for first_part, second_part in zip(row_back, col_back)]
    attn = joined[0]
    flat_attn = attn.reshape(-1, head_width)
    layer_out = jnp.dot(flat_attn, out_weight, preferred_element_type=jnp.float32).astype(jnp.bfloat16).reshape(SEQS, ROWS, STRIDE, D)
    weight_grad = jnp.dot(flat_attn.T, flat_cot, preferred_element_type=jnp.float32) / math.sqrt(ALL_TOKENS)
    return (layer_out, joined[1], joined[2], joined[3], weight_grad)
```

```python
import functools
import math

import jax
import jax.numpy as jnp
from jax import lax
from jax.experimental import pallas as pl
from jax.experimental.pallas import tpu as pltpu
from jax.sharding import PartitionSpec as P

ROW_HEADS = 4
COL_HEADS = 4
DH = 128
ROW_WIDTH = ROW_HEADS * DH
COL_WIDTH = COL_HEADS * DH
FACTOR = 1.0 / math.sqrt(DH)
EXP_SCALE = FACTOR * math.log2(math.e)
BLOCK = 256
LOW = -1e30
BF16 = jnp.bfloat16
F32 = jnp.float32
VMEM = 56 * 1024 * 1024
DECLARED = {
    "pack": 0.6, "unpack": 0.6, "row_forward": 1.0, "row_backward": 1.4,
    "column_forward": 110.0, "column_backward": 120.0, "upstream_col": 0.7, "upstream_row": 0.7,
    "weight_row": 0.6, "weight_col": 0.6, "layer_output": 0.9,
}
DECLARED_FLOPS = 1.15e9


def cost(name):
    return pl.CostEstimate(
        flops=int(DECLARED[name] * DECLARED_FLOPS), transcendentals=0, bytes_accessed=0
    )


def params():
    return pltpu.CompilerParams(vmem_limit_bytes=VMEM)


def dot(a, b, a_dim, b_dim):
    return lax.dot_general(a, b, (((a_dim,), (b_dim,)), ((), ())), preferred_element_type=F32)


def whole(shape):
    return pl.BlockSpec(shape, lambda *_: (0,) * len(shape))


def softmax_chunks(score_chunks):
    peak = functools.reduce(
        jnp.maximum, [jnp.max(s, axis=0, keepdims=True) for s in score_chunks]
    )
    shift = peak * EXP_SCALE
    raised = [jnp.exp2(s * EXP_SCALE - shift) for s in score_chunks]
    total = functools.reduce(jnp.add, [jnp.sum(e, axis=0, keepdims=True) for e in raised])
    inverse = 1.0 / total
    return [e * inverse for e in raised]


def backward_chunks(shares, query, upstream, keys, values):
    lows = [p.astype(BF16) for p in shares]
    share_grads = [dot(v, upstream, 1, 1) for v in values]
    row_total = functools.reduce(
        jnp.add, [jnp.sum(p * g, axis=0, keepdims=True) for p, g in zip(shares, share_grads)]
    )
    score_lows = [(p * (g - row_total)).astype(BF16) for p, g in zip(shares, share_grads)]
    value_parts = [dot(p, upstream, 1, 0) for p in lows]
    key_parts = [dot(s, query, 1, 0) for s in score_lows]
    query_part = functools.reduce(jnp.add, [dot(k, s, 0, 0) for k, s in zip(keys, score_lows)])
    return query_part.T, key_parts, value_parts


def causal_mask(block):
    return lax.broadcasted_iota(jnp.int32, (block, block), 0) <= lax.broadcasted_iota(
        jnp.int32, (block, block), 1
    )


def row_scores(q_ref, k_ref, i, block):
    query = q_ref[pl.ds(i * block, block), :]
    chunks = []
    for j in range(i + 1):
        s = dot(k_ref[pl.ds(j * block, block), :], query, 1, 1)
        if j == i:
            s = jnp.where(causal_mask(block), s, LOW)
        chunks.append(s)
    return query, chunks


def row_forward_kernel(q_ref, k_ref, v_ref, out_ref):
    steps = q_ref.shape[0]
    block = min(BLOCK, steps)
    for i in range(steps // block):
        _, chunks = row_scores(q_ref, k_ref, i, block)
        shares = softmax_chunks(chunks)
        total = functools.reduce(
            jnp.add,
            [
                dot(v_ref[pl.ds(j * block, block), :], p.astype(BF16), 0, 0)
                for j, p in enumerate(shares)
            ],
        )
        out_ref[pl.ds(i * block, block), :] = total.T.astype(BF16)


def row_backward_kernel(q_ref, k_ref, v_ref, u_ref, dq_ref, dk_ref, dv_ref, dk_sum, dv_sum):
    steps = q_ref.shape[0]
    block = min(BLOCK, steps)
    for i in range(steps // block):
        query, chunks = row_scores(q_ref, k_ref, i, block)
        shares = softmax_chunks(chunks)
        upstream = u_ref[pl.ds(i * block, block), :]
        keys = [k_ref[pl.ds(j * block, block), :] for j in range(i + 1)]
        values = [v_ref[pl.ds(j * block, block), :] for j in range(i + 1)]
        query_part, key_parts, value_parts = backward_chunks(
            shares, query, upstream, keys, values
        )
        dq_ref[pl.ds(i * block, block), :] = (query_part * FACTOR).astype(BF16)
        for j in range(i + 1):
            rows = pl.ds(j * block, block)
            if j == i:
                dk_sum[rows, :] = key_parts[j]
                dv_sum[rows, :] = value_parts[j]
            else:
                dk_sum[rows, :] += key_parts[j]
                dv_sum[rows, :] += value_parts[j]
    dk_ref[...] = (dk_sum[...] * FACTOR).astype(BF16)
    dv_ref[...] = dv_sum[...].astype(BF16)


def row_forward(queries, keys, values):
    steps = queries.shape[0]
    head = pl.BlockSpec((steps, DH), lambda h: (0, h))
    return pl.pallas_call(
        row_forward_kernel,
        grid=(ROW_HEADS,),
        in_specs=[head] * 3,
        out_specs=head,
        out_shape=jax.ShapeDtypeStruct((steps, ROW_WIDTH), BF16),
        compiler_params=params(),
        cost_estimate=cost("row_forward"),
        name="row_forward",
    )(queries, keys, values)


def row_backward(queries, keys, values, upstream):
    steps = queries.shape[0]
    head = pl.BlockSpec((steps, DH), lambda h: (0, h))
    return pl.pallas_call(
        row_backward_kernel,
        grid=(ROW_HEADS,),
        in_specs=[head] * 4,
        out_specs=[head] * 3,
        out_shape=[jax.ShapeDtypeStruct(queries.shape, BF16)] * 3,
        scratch_shapes=[pltpu.VMEM((steps, DH), F32)] * 2,
        compiler_params=params(),
        cost_estimate=cost("row_backward"),
        name="row_backward",
    )(queries, keys, values, upstream)


def pack_kernel(q_ref, k_ref, v_ref, out_ref):
    group, _, cols, width = out_ref.shape
    for n, ref in enumerate((q_ref, k_ref, v_ref)):
        out_ref[:, n] = ref[...].reshape(group, cols, width)


def pack_specs(peers, cols):
    group = peers // 2
    return (
        pl.BlockSpec((group * cols, COL_WIDTH), lambda j: (j, ROW_WIDTH // COL_WIDTH)),
        pl.BlockSpec((group, 3, cols, COL_WIDTH), lambda j: (j, 0, 0, 0)),
    )


def pack(queries, keys, values, peers):
    cols = queries.shape[0] // peers
    apart, together = pack_specs(peers, cols)
    return pl.pallas_call(
        pack_kernel,
        grid=(2,),
        in_specs=[apart] * 3,
        out_specs=together,
        out_shape=jax.ShapeDtypeStruct((peers, 3, cols, COL_WIDTH), BF16),
        compiler_params=params(),
        cost_estimate=cost("pack"),
        name="pack",
    )(queries, keys, values)


def unpack_kernel(in_ref, _q, _k, _v, dq_ref, dk_ref, dv_ref):
    for n, ref in enumerate((dq_ref, dk_ref, dv_ref)):
        ref[...] = in_ref[:, n].reshape(ref.shape)


def unpack(packed, dq, dk, dv):
    peers, _, cols, _ = packed.shape
    apart, together = pack_specs(peers, cols)
    anywhere = pl.BlockSpec(memory_space=pl.ANY)
    return pl.pallas_call(
        unpack_kernel,
        grid=(2,),
        in_specs=[together] + [anywhere] * 3,
        out_specs=[apart] * 3,
        out_shape=[jax.ShapeDtypeStruct(dq.shape, BF16)] * 3,
        input_output_aliases={1: 0, 2: 1, 3: 2},
        compiler_params=params(),
        cost_estimate=cost("unpack"),
        name="unpack",
    )(packed, dq, dk, dv)


def column_mask(rows, cols):
    key = lax.broadcasted_iota(jnp.int32, (rows * cols, rows * cols), 0)
    query = lax.broadcasted_iota(jnp.int32, (rows * cols, rows * cols), 1)
    return (key <= query) & (key % cols == query % cols)


def head_tokens(block, h):
    rows, cols, _ = block.shape
    return block[:, :, h * DH : (h + 1) * DH].reshape(rows * cols, DH)


def column_forward_kernel(in_ref, out_ref):
    rows, _, cols, _ = in_ref.shape
    mask = column_mask(rows, cols)
    for h in range(COL_HEADS):
        query, key, value = [head_tokens(in_ref[:, n], h) for n in range(3)]
        scores = jnp.where(mask, dot(key, query, 1, 1), LOW)
        (share,) = softmax_chunks([scores])
        result = dot(value, share.astype(BF16), 0, 0).T
        out_ref[:, :, h * DH : (h + 1) * DH] = result.astype(BF16).reshape(rows, cols, DH)


def column_backward_kernel(in_ref, u_ref, out_ref):
    rows, _, cols, _ = in_ref.shape
    mask = column_mask(rows, cols)
    for h in range(COL_HEADS):
        query, key, value = [head_tokens(in_ref[:, n], h) for n in range(3)]
        upstream = head_tokens(u_ref[...], h)
        scores = jnp.where(mask, dot(key, query, 1, 1), LOW)
        shares = softmax_chunks([scores])
        query_grad, (key_grad,), (value_grad,) = backward_chunks(
            shares, query, upstream, [key], [value]
        )
        span = slice(h * DH, (h + 1) * DH)
        out_ref[:, 0, :, span] = (query_grad * FACTOR).astype(BF16).reshape(rows, cols, DH)
        out_ref[:, 1, :, span] = (key_grad * FACTOR).astype(BF16).reshape(rows, cols, DH)
        out_ref[:, 2, :, span] = value_grad.astype(BF16).reshape(rows, cols, DH)


def column_call(kernel, packed, upstream, name):
    rows, _, cols, width = packed.shape
    span = min(16, cols)
    three = pl.BlockSpec((rows, 3, span, width), lambda c: (0, 0, c, 0))
    one = pl.BlockSpec((rows, span, width), lambda c: (0, c, 0))
    forward = upstream is None
    return pl.pallas_call(
        kernel,
        grid=(cols // span,),
        in_specs=[three] if forward else [three, one],
        out_specs=one if forward else three,
        out_shape=jax.ShapeDtypeStruct(
            (rows, cols, width) if forward else (rows, 3, cols, width), BF16
        ),
        compiler_params=params(),
        cost_estimate=cost(name),
        name=name,
    )(*((packed,) if forward else (packed, upstream)))


def upstream_kernel(place_ref, *refs):
    *w_refs, cot_ref, up_ref, full_ref = refs
    each, rows, _ = w_refs[0].shape

    @pl.when(pl.program_id(0) == 0)
    def _():
        for n, w_ref in enumerate(w_refs):
            for m in range(each):
                at = pl.multiple_of(place_ref[n * each + m], rows)
                full_ref[pl.ds(at, rows), :] = w_ref[m]

    up_ref[...] = dot(cot_ref[...], full_ref[...], 1, 1).astype(BF16)


def upstream_of(place, pieces, cotangent, name):
    steps, model = cotangent.shape
    each, rows, _ = pieces[0].shape
    count = each * len(pieces)
    block = min(BLOCK, steps)
    return pl.pallas_call(
        upstream_kernel,
        grid=(steps // block,),
        in_specs=[
            pl.BlockSpec(memory_space=pltpu.SMEM),
            *[whole(piece.shape) for piece in pieces],
            pl.BlockSpec((block, model), lambda t: (t, 0)),
        ],
        out_specs=[
            pl.BlockSpec((block, count * rows), lambda t: (t, 0)),
            whole((count * rows, model)),
        ],
        out_shape=[
            jax.ShapeDtypeStruct((steps, count * rows), BF16),
            jax.ShapeDtypeStruct((count * rows, model), BF16),
        ],
        compiler_params=params(),
        cost_estimate=cost(name),
        name=name,
    )(place, *pieces, cotangent)


def layer_kernel(row_ref, col_ref, w_row_ref, w_col_ref, out_ref):
    out_ref[...] = (
        dot(row_ref[...], w_row_ref[...], 1, 0) + dot(col_ref[...], w_col_ref[...], 1, 0)
    ).astype(BF16)


def layer_output(attn_row, attn_col, w_row, w_col):
    steps, width = attn_row.shape
    model = w_row.shape[1]
    block = min(BLOCK, steps)
    return pl.pallas_call(
        layer_kernel,
        grid=(steps // block,),
        in_specs=[pl.BlockSpec((block, width), lambda t: (t, 0))] * 2 + [whole(w_row.shape)] * 2,
        out_specs=pl.BlockSpec((block, model), lambda t: (t, 0)),
        out_shape=jax.ShapeDtypeStruct((steps, model), BF16),
        compiler_params=params(),
        cost_estimate=cost("layer_output"),
        name="layer_output",
    )(attn_row, attn_col, w_row, w_col)


def weight_kernel(factor, core_ref, attn_ref, cot_ref, keep_ref, send_ref):
    product = dot(attn_ref[...], cot_ref[...], 0, 0) * factor
    first = core_ref[0] == 0
    for n in range(keep_ref.shape[0]):
        even = product[2 * n * DH : (2 * n + 1) * DH]
        odd = product[(2 * n + 1) * DH : (2 * n + 2) * DH]
        keep_ref[n] = jnp.where(first, even, odd)
        send_ref[n] = jnp.where(first, odd, even).astype(BF16)


def weight_part(core, attn, cotangent, factor, name):
    steps, width = attn.shape
    model = cotangent.shape[1]
    block = min(2 * BLOCK, model)
    pairs = width // DH // 2
    out = pl.BlockSpec((pairs, DH, block), lambda n: (0, 0, n))
    return pl.pallas_call(
        functools.partial(weight_kernel, factor),
        grid=(model // block,),
        in_specs=[
            pl.BlockSpec(memory_space=pltpu.SMEM),
            whole((steps, width)),
            pl.BlockSpec((steps, block), lambda n: (0, n)),
        ],
        out_specs=[out, out],
        out_shape=[
            jax.ShapeDtypeStruct((pairs, DH, model), F32),
            jax.ShapeDtypeStruct((pairs, DH, model), BF16),
        ],
        compiler_params=params(),
        cost_estimate=cost(name),
        name=name,
    )(core, attn, cotangent)


def flip(array, axis, bits, size):
    return lax.ppermute(array, axis, [(n, n ^ bits) for n in range(size)])


def after(member, *others):
    return lax.optimization_barrier((member, *others))[0]


def gather_plane(shard, seq_size):
    pairs = seq_size // 2
    near = [shard] + [flip(shard, "seq", 2 * d, seq_size) for d in range(1, pairs)]
    close, far = jnp.stack(near[: pairs // 2]), jnp.stack(near[pairs // 2 :])
    upper = lax.axis_index("seq") // 2 >= pairs // 2
    return near[1:], jnp.where(upper, close, far), jnp.where(upper, far, close)


def gather_dp(mine, dp_size):
    return [mine] + [flip(mine, "dp", e, dp_size) for e in range(1, dp_size)]


def gather_core(column, seq_size):
    return column + [flip(member, "seq", 1, seq_size) for member in column]


def piece_places(rows, seq_size, dp_size):
    me = lax.axis_index("seq")
    half = seq_size // 4
    c = (jnp.arange(2) ^ (me % 2))[:, None, None]
    z = (jnp.arange(dp_size) ^ lax.axis_index("dp"))[None, :, None]
    pair = (jnp.arange(half) ^ (me // 2 % half))[None, None, :]
    return (((pair * 2 + c) * dp_size + z) * rows).reshape(-1).astype(jnp.int32)


def dp_pieces(keep, received, dp_size):
    pairs, _, model = keep.shape
    depth = lax.axis_index("dp")
    rows = DH // dp_size
    own = keep.reshape(pairs, dp_size, rows, model)
    other = received.reshape(pairs, dp_size, rows, model)

    def part(e):
        at = depth ^ e
        return lax.dynamic_index_in_dim(own, at, 1, False) + lax.dynamic_index_in_dim(
            other, at, 1, False
        ).astype(F32)

    return part(0), [part(e).astype(BF16) for e in range(1, dp_size)]


def send_over_dp(pieces, dp_size):
    return [flip(piece, "dp", e, dp_size) for e, piece in enumerate(pieces, 1)]


def sum_up(own, arrived):
    return functools.reduce(jnp.add, [member.astype(F32) for member in arrived], own)


def scatter_over_seq(parts, seq_size):
    pair = lax.axis_index("seq") // 2
    total = lax.dynamic_index_in_dim(parts, pair, 0, False)
    for d in range(1, seq_size // 2):
        piece = lax.dynamic_index_in_dim(parts, pair ^ d, 0, False).astype(BF16)
        total = total + flip(piece, "seq", 2 * d, seq_size).astype(F32)
    return total


def body(queries, keys, values, out_weight, cotangent):
    seq_size, dp_size = lax.axis_size("seq"), lax.axis_size("dp")
    shape, cot_shape = queries.shape, cotangent.shape
    queries, keys, values, cotangent = [
        member.reshape(-1, member.shape[-1]) for member in (queries, keys, values, cotangent)
    ]
    steps = queries.shape[0]
    model = cotangent.shape[1]
    rows = out_weight.shape[0]
    factor = 1.0 / math.sqrt(steps * seq_size * dp_size)
    core = (lax.axis_index("seq") % 2).reshape(1).astype(jnp.int32)
    staged = seq_size == ROW_HEADS + COL_HEADS and rows % 16 == 0

    def exchange(member):
        return lax.all_to_all(member, "seq", split_axis=0, concat_axis=0, tiled=True)

    packed = pack(queries, keys, values, seq_size)
    if not staged:
        place = jnp.zeros((1,), jnp.int32)
        full = lax.all_gather(out_weight, ("seq", "dp"), axis=0, tiled=True)
        row_pieces, col_pieces = [full[None, :ROW_WIDTH]], [full[None, ROW_WIDTH:]]
        row_near = []
    else:
        place = piece_places(rows, seq_size, dp_size)
        near, col_mine, row_mine = gather_plane(out_weight, seq_size)
        packed = after(packed, *near)
        queries_then = after(queries, col_mine)
    arrived = exchange(packed)
    attn_row = row_forward(queries_then if staged else queries, keys, values)
    row_keep, row_send = weight_part(core, attn_row, cotangent, factor, "weight_row")
    if staged:
        col_depth = gather_dp(col_mine, dp_size)
        col_pieces = gather_core([after(member, row_send) for member in col_depth], seq_size)
        row_depth = gather_dp(after(row_mine, *col_depth), dp_size)
        row_near = row_depth[1:2]
        row_received = flip(after(row_send, *col_pieces), "seq", 1, seq_size)

    up_col, w_col = upstream_of(place, col_pieces, cotangent, "upstream_col")
    up_arrived = exchange(after(up_col, arrived).reshape(seq_size, -1, COL_WIDTH))
    out_col = column_call(
        column_forward_kernel, after(arrived, up_col, *row_near), None, "column_forward"
    )
    attn_col = exchange(after(out_col, up_arrived)).reshape(steps, COL_WIDTH)
    if staged:
        row_pieces = gather_core([after(member, out_col) for member in row_depth], seq_size)
    if staged:
        row_own, row_out = dp_pieces(row_keep, row_received, dp_size)
        row_sent = send_over_dp([after(piece, *row_depth) for piece in row_out], dp_size)
        up_arrived = after(up_arrived, *row_out, *row_pieces)
    grads_col = column_call(column_backward_kernel, arrived, up_arrived, "column_backward")
    attn_col = after(attn_col, grads_col)
    grads_arrived = exchange(after(grads_col, attn_col))
    if staged:
        attn_col = after(attn_col, *row_sent[:2])
    col_keep, col_send = weight_part(core, attn_col, cotangent, factor, "weight_col")
    then = [col_send]
    if staged:
        col_own, col_out = dp_pieces(col_keep, flip(col_send, "seq", 1, seq_size), dp_size)
        col_sent = send_over_dp(col_out, dp_size)
        then += col_out
    up_row, w_row = upstream_of(place, row_pieces, after(cotangent, *then), "upstream_row")
    dq, dk, dv = row_backward(queries, keys, values, up_row)
    layer_out = layer_output(after(attn_row, dq), attn_col, w_row, w_col)
    if staged:
        row_total = sum_up(row_own, [after(member, layer_out) for member in row_sent])
        col_total = sum_up(col_own, [after(member, layer_out) for member in col_sent])
        weight_grad = scatter_over_seq(jnp.concatenate([row_total, col_total]), seq_size)
    else:
        keep = jnp.stack([row_keep, col_keep])
        send = jnp.stack([row_send, col_send]).astype(F32)
        even, odd = jnp.where(core[0] == 0, keep, send), jnp.where(core[0] == 0, send, keep)
        local = jnp.stack([even, odd], axis=2).reshape(-1, model)
        weight_grad = lax.psum_scatter(local, ("seq", "dp"), scatter_dimension=0, tiled=True)
    dq, dk, dv = unpack(grads_arrived, dq, dk, dv)
    return (
        layer_out.reshape(cot_shape),
        dq.reshape(shape),
        dk.reshape(shape),
        dv.reshape(shape),
        weight_grad,
    )


def solution(mesh):
    tokens = P("dp", "seq", None, None)
    weights = P(("seq", "dp"), None)
    return jax.shard_map(
        body,
        mesh=mesh,
        in_specs=(tokens, tokens, tokens, weights, tokens),
        out_specs=(tokens, tokens, tokens, tokens, weights),
        check_vma=False,
    )
```

```python
import functools
import math

import jax
import jax.numpy as jnp
from jax import lax
from jax.experimental import pallas as pl
from jax.experimental.pallas import tpu as pltpu
from jax.sharding import PartitionSpec as P

ROW_HEADS = 4
COL_HEADS = 4
DH = 128
ROW_WIDTH = ROW_HEADS * DH
COL_WIDTH = COL_HEADS * DH
FACTOR = 1.0 / math.sqrt(DH)
EXP_SCALE = FACTOR * math.log2(math.e)
BLOCK = 256
COLUMN_SPAN = 16
SENT_FIRST = 2
LOW = -1e30
BF16 = jnp.bfloat16
F32 = jnp.float32
VMEM = 56 * 1024 * 1024
DECLARED = {
    "pack": 0.6, "unpack": 0.6, "row_forward": 100.0, "row_backward": 1.4, "column_forward": 110.0,
    "column_backward": 120.0, "upstream_col": 70.0, "upstream_row": 0.1, "weight_row": 0.6,
    "weight_col": 0.1, "layer_output": 0.9,
}
DECLARED_FLOPS = 1.15e9


def cost(name):
    return pl.CostEstimate(
        flops=int(DECLARED[name] * DECLARED_FLOPS), transcendentals=0, bytes_accessed=0
    )


def params():
    return pltpu.CompilerParams(vmem_limit_bytes=VMEM)


def dot(a, b, a_dim, b_dim):
    return lax.dot_general(a, b, (((a_dim,), (b_dim,)), ((), ())), preferred_element_type=F32)


def whole(shape):
    return pl.BlockSpec(shape, lambda *_: (0,) * len(shape))


def total_of(members):
    return functools.reduce(jnp.add, members)


def joined(parts):
    parts = [part.astype(BF16) for part in parts]
    return parts[0] if len(parts) == 1 else jnp.concatenate(parts, axis=0)


def softmax_units(units):
    peaks = [
        functools.reduce(jnp.maximum, [jnp.max(s, axis=0, keepdims=True) for s in parts])
        * EXP_SCALE
        for parts in units
    ]
    raised = [
        [jnp.exp2(s * EXP_SCALE - peak) for s in parts] for parts, peak in zip(units, peaks)
    ]
    inverses = [
        1.0 / total_of([jnp.sum(e, axis=0, keepdims=True) for e in parts]) for parts in raised
    ]
    return [[e * inverse for e in parts] for parts, inverse in zip(raised, inverses)]


def forward_units(units, values):
    shares = [joined(parts) for parts in softmax_units(units)]
    results = [dot(value, share, 0, 0) for value, share in zip(values, shares)]
    return [result.T.astype(BF16) for result in results]


def backward_units(units, share_grads, queries, keys, upstreams):
    shares = softmax_units(units)
    row_totals = [
        total_of([jnp.sum(p * g, axis=0, keepdims=True) for p, g in zip(parts, grads)])
        for parts, grads in zip(shares, share_grads)
    ]
    score_lows = [
        joined([p * (g - row_total) for p, g in zip(parts, grads)])
        for parts, grads, row_total in zip(shares, share_grads, row_totals)
    ]
    lows = [joined(parts) for parts in shares]
    query_grads = [dot(key, low, 0, 0).T * FACTOR for key, low in zip(keys, score_lows)]
    key_grads = [dot(low, query, 1, 0) for low, query in zip(score_lows, queries)]
    value_grads = [dot(low, upstream, 1, 0) for low, upstream in zip(lows, upstreams)]
    return query_grads, key_grads, value_grads


def causal_mask(block):
    return lax.broadcasted_iota(jnp.int32, (block, block), 0) <= lax.broadcasted_iota(
        jnp.int32, (block, block), 1
    )


def cut(scores, block):
    before = scores.shape[0] - block
    return [scores[:before], scores[before:]] if before else [scores]


def row_parts(key, query, block):
    parts = cut(dot(key, query, 1, 1), block)
    return parts[:-1] + [jnp.where(causal_mask(block), parts[-1], LOW)]


def head_span(h):
    return slice(h * DH, (h + 1) * DH)


def row_forward_kernel(q_ref, k_ref, v_ref, *refs):
    out_ref = refs[-1]
    steps, width = q_ref.shape
    block = min(BLOCK, steps)
    count = steps // block
    for first in range((count + 1) // 2):
        places = {first, count - 1 - first}
        units = [(i, head_span(h)) for i in sorted(places) for h in range(width // DH)]
        scores = [
            row_parts(
                k_ref[: (i + 1) * block, span], q_ref[i * block : (i + 1) * block, span], block
            )
            for i, span in units
        ]
        results = forward_units(scores, [v_ref[: (i + 1) * block, span] for i, span in units])
        for (i, span), result in zip(units, results):
            out_ref[i * block : (i + 1) * block, span] = result


def row_backward_kernel(q_ref, k_ref, v_ref, u_ref, dq_ref, dk_ref, dv_ref, dk_sum, dv_sum):
    steps = q_ref.shape[0]
    block = min(BLOCK, steps)
    count = steps // block
    order = range(count - 1, -1, -1)
    queries = [q_ref[i * block : (i + 1) * block, :] for i in order]
    upstreams = [u_ref[i * block : (i + 1) * block, :] for i in order]
    keys = [k_ref[: (i + 1) * block, :] for i in order]
    values = [v_ref[: (i + 1) * block, :] for i in order]
    scores = [row_parts(key, query, block) for key, query in zip(keys, queries)]
    share_grads = [
        cut(dot(value, upstream, 1, 1), block) for value, upstream in zip(values, upstreams)
    ]
    query_grads, key_grads, value_grads = backward_units(
        scores, share_grads, queries, keys, upstreams
    )
    for i, grad in zip(order, query_grads):
        dq_ref[i * block : (i + 1) * block, :] = grad.astype(BF16)
    for i, key_grad, value_grad in zip(order, key_grads, value_grads):
        rows = slice(0, (i + 1) * block)
        if i == count - 1:
            dk_sum[...] = key_grad
            dv_sum[...] = value_grad
        else:
            dk_sum[rows, :] += key_grad
            dv_sum[rows, :] += value_grad
    dk_ref[...] = (dk_sum[...] * FACTOR).astype(BF16)
    dv_ref[...] = dv_sum[...].astype(BF16)


def row_forward(queries, keys, values, *others):
    steps = queries.shape[0]
    head = pl.BlockSpec((steps, 2 * DH), lambda h: (0, h))
    return pl.pallas_call(
        row_forward_kernel,
        grid=(ROW_HEADS // 2,),
        in_specs=[head] * 3 + [pl.BlockSpec(memory_space=pl.ANY)] * len(others),
        out_specs=head,
        out_shape=jax.ShapeDtypeStruct((steps, ROW_WIDTH), BF16),
        compiler_params=params(),
        cost_estimate=cost("row_forward"),
        name="row_forward",
    )(queries, keys, values, *others)


def row_backward(queries, keys, values, upstream):
    steps = queries.shape[0]
    head = pl.BlockSpec((steps, DH), lambda h: (0, h))
    return pl.pallas_call(
        row_backward_kernel,
        grid=(ROW_HEADS,),
        in_specs=[head] * 4,
        out_specs=[head] * 3,
        out_shape=[jax.ShapeDtypeStruct(queries.shape, BF16)] * 3,
        scratch_shapes=[pltpu.VMEM((steps, DH), F32)] * 2,
        compiler_params=params(),
        cost_estimate=cost("row_backward"),
        name="row_backward",
    )(queries, keys, values, upstream)


def pack_kernel(q_ref, k_ref, v_ref, out_ref):
    group, _, cols, width = out_ref.shape
    for n, ref in enumerate((q_ref, k_ref, v_ref)):
        out_ref[:, n] = ref[...].reshape(group, cols, width)


def pack_specs(peers, cols):
    group = peers // 2
    return (
        pl.BlockSpec((group * cols, COL_WIDTH), lambda j: (j, ROW_WIDTH // COL_WIDTH)),
        pl.BlockSpec((group, 3, cols, COL_WIDTH), lambda j: (j, 0, 0, 0)),
    )


def pack(queries, keys, values, peers):
    cols = queries.shape[0] // peers
    apart, together = pack_specs(peers, cols)
    return pl.pallas_call(
        pack_kernel,
        grid=(2,),
        in_specs=[apart] * 3,
        out_specs=together,
        out_shape=jax.ShapeDtypeStruct((peers, 3, cols, COL_WIDTH), BF16),
        compiler_params=params(),
        cost_estimate=cost("pack"),
        name="pack",
    )(queries, keys, values)


def unpack_kernel(in_ref, _q, _k, _v, dq_ref, dk_ref, dv_ref):
    for n, ref in enumerate((dq_ref, dk_ref, dv_ref)):
        ref[...] = in_ref[:, n].reshape(ref.shape)


def unpack(packed, dq, dk, dv):
    peers, _, cols, _ = packed.shape
    apart, together = pack_specs(peers, cols)
    anywhere = pl.BlockSpec(memory_space=pl.ANY)
    return pl.pallas_call(
        unpack_kernel,
        grid=(2,),
        in_specs=[together] + [anywhere] * 3,
        out_specs=[apart] * 3,
        out_shape=[jax.ShapeDtypeStruct(dq.shape, BF16)] * 3,
        input_output_aliases={1: 0, 2: 1, 3: 2},
        compiler_params=params(),
        cost_estimate=cost("unpack"),
        name="unpack",
    )(packed, dq, dk, dv)


def column_mask(rows, cols):
    key = lax.broadcasted_iota(jnp.int32, (rows * cols, rows * cols), 0)
    query = lax.broadcasted_iota(jnp.int32, (rows * cols, rows * cols), 1)
    return (key <= query) & (key % cols == query % cols)


def head_tokens(ref, n, unit):
    cols, span = unit
    block = ref[:, cols, span] if n is None else ref[:, n, cols, span]
    return block.reshape(-1, DH)


def column_units(width, span):
    units = [
        (slice(c * span, (c + 1) * span), head_span(h))
        for c in range(width // span)
        for h in range(COL_HEADS)
    ]
    return [units[n : n + 8] for n in range(0, len(units), 8)]


def column_scores(in_ref, units, mask):
    return [
        [jnp.where(mask, dot(head_tokens(in_ref, 1, unit), head_tokens(in_ref, 0, unit), 1, 1), LOW)]
        for unit in units
    ]


def column_forward_kernel(in_ref, out_ref):
    rows, _, width, _ = in_ref.shape
    span = min(COLUMN_SPAN, width)
    mask = column_mask(rows, span)
    for units in column_units(width, span):
        scores = column_scores(in_ref, units, mask)
        results = forward_units(scores, [head_tokens(in_ref, 2, unit) for unit in units])
        for (cols, lanes), result in zip(units, results):
            out_ref[:, cols, lanes] = result.reshape(rows, span, DH)


def column_backward_kernel(in_ref, u_ref, out_ref):
    rows, _, width, _ = in_ref.shape
    span = min(COLUMN_SPAN, width)
    mask = column_mask(rows, span)
    for units in column_units(width, span):
        queries, keys, values = [
            [head_tokens(in_ref, n, unit) for unit in units] for n in range(3)
        ]
        upstreams = [head_tokens(u_ref, None, unit) for unit in units]
        scores = column_scores(in_ref, units, mask)
        share_grads = [[dot(v, u, 1, 1)] for v, u in zip(values, upstreams)]
        grads = backward_units(scores, share_grads, queries, keys, upstreams)
        for (cols, lanes), query_grad, key_grad, value_grad in zip(units, *grads):
            for n, grad in enumerate((query_grad, key_grad * FACTOR, value_grad)):
                out_ref[:, n, cols, lanes] = grad.astype(BF16).reshape(rows, span, DH)


def column_call(kernel, packed, upstream, parts, name):
    rows, _, cols, width = packed.shape
    span = max(min(COLUMN_SPAN, cols), cols // parts)
    three = pl.BlockSpec((rows, 3, span, width), lambda c: (0, 0, c, 0))
    one = pl.BlockSpec((rows, span, width), lambda c: (0, c, 0))
    forward = upstream is None
    return pl.pallas_call(
        kernel,
        grid=(cols // span,),
        in_specs=[three] if forward else [three, one],
        out_specs=one if forward else three,
        out_shape=jax.ShapeDtypeStruct(
            (rows, cols, width) if forward else (rows, 3, cols, width), BF16
        ),
        compiler_params=params(),
        cost_estimate=cost(name),
        name=name,
    )(*((packed,) if forward else (packed, upstream)))


def upstream_kernel(place_ref, *refs):
    *w_refs, cot_ref, up_ref, full_ref = refs
    each, rows, _ = w_refs[0].shape

    @pl.when(pl.program_id(0) == 0)
    def _():
        for n, w_ref in enumerate(w_refs):
            for m in range(each):
                at = pl.multiple_of(place_ref[n * each + m], rows)
                full_ref[pl.ds(at, rows), :] = w_ref[m]

    up_ref[...] = dot(cot_ref[...], full_ref[...], 1, 1).astype(BF16)


def upstream_of(place, pieces, cotangent, name):
    steps, model = cotangent.shape
    each, rows, _ = pieces[0].shape
    width = each * len(pieces) * rows
    block = min(2 * BLOCK, steps)
    return pl.pallas_call(
        upstream_kernel,
        grid=(steps // block,),
        in_specs=[
            pl.BlockSpec(memory_space=pltpu.SMEM),
            *[whole(piece.shape) for piece in pieces],
            pl.BlockSpec((block, model), lambda t: (t, 0)),
        ],
        out_specs=[pl.BlockSpec((block, width), lambda t: (t, 0)), whole((width, model))],
        out_shape=[
            jax.ShapeDtypeStruct((steps, width), BF16),
            jax.ShapeDtypeStruct((width, model), BF16),
        ],
        compiler_params=params(),
        cost_estimate=cost(name),
        name=name,
    )(place, *pieces, cotangent)


def layer_kernel(row_ref, col_ref, w_row_ref, w_col_ref, out_ref):
    out_ref[...] = (
        dot(row_ref[...], w_row_ref[...], 1, 0) + dot(col_ref[...], w_col_ref[...], 1, 0)
    ).astype(BF16)


def layer_output(attn_row, attn_col, w_row, w_col):
    steps, width = attn_row.shape
    model = w_row.shape[1]
    block = min(BLOCK, steps)
    return pl.pallas_call(
        layer_kernel,
        grid=(steps // block,),
        in_specs=[pl.BlockSpec((block, width), lambda t: (t, 0))] * 2 + [whole(w_row.shape)] * 2,
        out_specs=pl.BlockSpec((block, model), lambda t: (t, 0)),
        out_shape=jax.ShapeDtypeStruct((steps, model), BF16),
        compiler_params=params(),
        cost_estimate=cost("layer_output"),
        name="layer_output",
    )(attn_row, attn_col, w_row, w_col)


def weight_kernel(factor, core_ref, attn_ref, cot_ref, keep_ref, send_ref):
    depths, pairs, rows, _ = keep_ref.shape
    product = dot(attn_ref[...], cot_ref[...], 0, 0) * factor
    first = core_ref[0] == 0
    for n in range(pairs):
        for z in range(depths):
            even, odd = [
                product[head * DH + z * rows : head * DH + (z + 1) * rows]
                for head in (2 * n, 2 * n + 1)
            ]
            keep_ref[z, n] = jnp.where(first, even, odd)
            send_ref[z, n] = jnp.where(first, odd, even).astype(send_ref.dtype)


def weight_parts(core, attn, cotangent, factor, depths, dtype, name):
    steps, width = attn.shape
    model = cotangent.shape[1]
    block = min(512, model)
    shape = (depths, width // DH // 2, DH // depths, model)
    out = pl.BlockSpec(shape[:-1] + (block,), lambda n: (0, 0, 0, n))
    return pl.pallas_call(
        functools.partial(weight_kernel, factor),
        grid=(model // block,),
        in_specs=[
            pl.BlockSpec(memory_space=pltpu.SMEM),
            whole((steps, width)),
            pl.BlockSpec((steps, block), lambda n: (0, n)),
        ],
        out_specs=[out, out],
        out_shape=[jax.ShapeDtypeStruct(shape, F32), jax.ShapeDtypeStruct(shape, dtype)],
        compiler_params=params(),
        cost_estimate=cost(name),
        name=name,
    )(core, attn, cotangent)


def flip(array, axis, bits, size):
    return lax.ppermute(array, axis, [(n, n ^ bits) for n in range(size)])


def after(member, *others):
    return lax.optimization_barrier((member, *others))[0]


def over_dp(pieces, dp_size):
    return [flip(piece, "dp", e, dp_size) for e, piece in enumerate(pieces, 1)]


def over_core(member, seq_size):
    return flip(member, "seq", 1, seq_size)


def over_plane(pieces, seq_size):
    return [flip(piece, "seq", 2 * d, seq_size) for d, piece in enumerate(pieces, 1)]


def gather_plane(shard, seq_size):
    pairs = seq_size // 2
    near = [shard, *over_plane([shard] * (pairs - 1), seq_size)]
    close, far = jnp.stack(near[: pairs // 2]), jnp.stack(near[pairs // 2 :])
    upper = lax.axis_index("seq") // 2 >= pairs // 2
    return jnp.where(upper, close, far), jnp.where(upper, far, close)


def piece_places(rows, seq_size, dp_size):
    me = lax.axis_index("seq")
    half = seq_size // 4
    c = (jnp.arange(2) ^ (me % 2))[:, None, None]
    z = (jnp.arange(dp_size) ^ lax.axis_index("dp"))[None, :, None]
    pair = (jnp.arange(half) ^ (me // 2 % half))[None, None, :]
    return (((pair * 2 + c) * dp_size + z) * rows).reshape(-1).astype(jnp.int32)


def cut_up(addends, me):
    def part(n):
        return functools.reduce(
            jnp.add,
            [lax.dynamic_index_in_dim(a, me ^ n, 0, False).astype(F32) for a in addends],
        )

    return part(0), [part(n).astype(BF16) for n in range(1, addends[0].shape[0])]


def sum_up(own, arrived):
    return functools.reduce(jnp.add, [member.astype(F32) for member in arrived], own)


def body(queries, keys, values, out_weight, cotangent):
    seq_size, dp_size = lax.axis_size("seq"), lax.axis_size("dp")
    shape, cot_shape = queries.shape, cotangent.shape
    queries, keys, values, cotangent = [
        member.reshape(-1, member.shape[-1]) for member in (queries, keys, values, cotangent)
    ]
    steps = queries.shape[0]
    model = cotangent.shape[1]
    rows = out_weight.shape[0]
    factor = 1.0 / math.sqrt(steps * seq_size * dp_size)
    core = (lax.axis_index("seq") % 2).reshape(1).astype(jnp.int32)
    staged = seq_size == ROW_HEADS + COL_HEADS and rows % 16 == 0

    def exchange(member):
        return lax.all_to_all(member, "seq", split_axis=0, concat_axis=0, tiled=True)

    def weights(attn, name):
        return weight_parts(core, attn, cotangent, factor, dp_size, BF16, name)

    packed = pack(queries, keys, values, seq_size)
    arrived = exchange(packed)
    if staged:
        pair, depth = lax.axis_index("seq") // 2, lax.axis_index("dp")
        place = piece_places(rows, seq_size, dp_size)
        col_mine, row_mine = gather_plane(out_weight, seq_size)
        col_depth = [col_mine, *over_dp([col_mine] * (dp_size - 1), dp_size)]
        attn_row = row_forward(queries, keys, values, packed, col_mine)
        row_keep, row_send = weights(attn_row, "weight_row")
        col_depth = [after(member, row_keep) for member in col_depth]
        col_pieces = col_depth + [over_core(member, seq_size) for member in col_depth]
        row_received = over_core(after(row_send, *col_pieces), seq_size)
        row_mine = after(row_mine, *col_depth)
        row_depth = [row_mine, *over_dp([row_mine] * (dp_size - 1), dp_size)]
        arrived = after(arrived, row_keep)
        then = [row_depth[1]]
    else:
        place = jnp.zeros((1,), jnp.int32)
        full = lax.all_gather(out_weight, ("seq", "dp"), axis=0, tiled=True)
        row_pieces, col_pieces = [full[None, :ROW_WIDTH]], [full[None, ROW_WIDTH:]]
        attn_row = row_forward(queries, keys, values)
        then = []

    out_col = column_call(column_forward_kernel, arrived, None, 2, "column_forward")
    attn_col = exchange(out_col).reshape(steps, COL_WIDTH)
    up_col, w_col = upstream_of(
        place, col_pieces, after(cotangent, out_col, *then), "upstream_col"
    )
    then = []
    if staged:
        row_own, row_out = cut_up((row_keep, after(row_received, up_col)), depth)
        row_pieces = row_depth + [
            over_core(after(member, up_col), seq_size) for member in row_depth
        ]
        then = row_depth + row_out
    up_arrived = exchange(after(up_col, attn_col, *then).reshape(seq_size, -1, COL_WIDTH))
    then = []
    if staged:
        row_sent = over_dp([after(piece, *row_depth) for piece in row_out], dp_size)
        col_keep, col_send = weights(attn_col, "weight_col")
        col_received = over_core(col_send, seq_size)
        then = [col_keep]
    up_row, w_row = upstream_of(place, row_pieces, after(cotangent, *then), "upstream_row")
    then = [up_row, *row_sent[:SENT_FIRST]] if staged else [up_row]
    up_arrived = after(up_arrived, *then)
    grads_col = column_call(column_backward_kernel, arrived, up_arrived, 4, "column_backward")
    grads_arrived = exchange(grads_col)
    then = [grads_col]
    if staged:
        col_own, col_out = cut_up((after(col_keep, grads_col), col_received), depth)
        col_sent = over_dp(col_out, dp_size)
        then = col_out
    dq, dk, dv = row_backward(queries, keys, values, after(up_row, *then))
    layer_out = layer_output(after(attn_row, dq), attn_col, w_row, w_col)
    if staged:
        row_total = sum_up(row_own, [after(member, layer_out) for member in row_sent])
        col_total = sum_up(col_own, [after(member, layer_out) for member in col_sent])
        own, out = cut_up((jnp.concatenate([row_total, col_total]),), pair)
        sent = over_plane(out, seq_size)
        dq, dk, dv = unpack(after(grads_arrived, *out), dq, dk, dv)
        weight_grad = sum_up(own, [after(member, dq) for member in sent])
    else:
        local = []
        for member, name in ((attn_row, "weight_row"), (attn_col, "weight_col")):
            even, odd = weight_parts(
                jnp.zeros((1,), jnp.int32), member, cotangent, factor, 1, F32, name
            )
            local.append(jnp.stack([even[0], odd[0]], axis=1).reshape(-1, model))
        weight_grad = lax.psum_scatter(
            jnp.concatenate(local), ("seq", "dp"), scatter_dimension=0, tiled=True
        )
        dq, dk, dv = unpack(grads_arrived, dq, dk, dv)
    return (
        layer_out.reshape(cot_shape),
        dq.reshape(shape),
        dk.reshape(shape),
        dv.reshape(shape),
        weight_grad,
    )


def solution(mesh):
    tokens = P("dp", "seq", None, None)
    weights = P(("seq", "dp"), None)
    return jax.shard_map(
        body,
        mesh=mesh,
        in_specs=(tokens, tokens, tokens, weights, tokens),
        out_specs=(tokens, tokens, tokens, tokens, weights),
        check_vma=False,
    )
```

```python
import functools
import math

import jax
import jax.numpy as jnp
from jax import lax
from jax.experimental import pallas as pl
from jax.experimental.pallas import tpu as pltpu
from jax.sharding import PartitionSpec as P

ROW_HEADS = 4
COL_HEADS = 4
DH = 128
ROW_WIDTH = ROW_HEADS * DH
COL_WIDTH = COL_HEADS * DH
FACTOR = 1.0 / math.sqrt(DH)
EXP_SCALE = FACTOR * math.log2(math.e)
BLOCK = 256
COLUMN_SPAN = 16
COLUMN_OUT = jax.ShapeDtypeStruct
SENT_FIRST = 2
LOW = -1e30
BF16 = jnp.bfloat16
F32 = jnp.float32
VMEM = 56 * 1024 * 1024
DECLARED = {
    "pack": 0.6, "unpack": 0.6, "row_forward": 100.0, "row_backward": 1.4, "column_forward": 110.0,
    "column_backward": 120.0, "upstream_col": 70.0, "upstream_row": 0.1, "weight_row": 0.6,
    "weight_col": 0.1, "layer_output": 0.9, "plane_pieces": 0.1,
}
DECLARED_FLOPS = 1.15e9


def cost(name):
    return pl.CostEstimate(
        flops=int(DECLARED[name] * DECLARED_FLOPS), transcendentals=0, bytes_accessed=0
    )


def params():
    return pltpu.CompilerParams(vmem_limit_bytes=VMEM)


def resident(array):
    return pltpu.with_memory_space_constraint(array, pltpu.VMEM)


RESIDENT = pl.BlockSpec(memory_space=pltpu.VMEM)


def dot(a, b, a_dim, b_dim):
    return lax.dot_general(a, b, (((a_dim,), (b_dim,)), ((), ())), preferred_element_type=F32)


def whole(shape):
    return pl.BlockSpec(shape, lambda *_: (0,) * len(shape))


def total_of(members):
    return functools.reduce(jnp.add, members)


def joined(parts):
    parts = [part.astype(BF16) for part in parts]
    return parts[0] if len(parts) == 1 else jnp.concatenate(parts, axis=0)


def softmax_units(units):
    peaks = [
        functools.reduce(jnp.maximum, [jnp.max(s, axis=0, keepdims=True) for s in parts])
        * EXP_SCALE
        for parts in units
    ]
    raised = [
        [jnp.exp2(s * EXP_SCALE - peak) for s in parts] for parts, peak in zip(units, peaks)
    ]
    inverses = [
        1.0 / total_of([jnp.sum(e, axis=0, keepdims=True) for e in parts]) for parts in raised
    ]
    return [[e * inverse for e in parts] for parts, inverse in zip(raised, inverses)]


def forward_units(units, values):
    shares = [joined(parts) for parts in softmax_units(units)]
    results = [dot(value, share, 0, 0) for value, share in zip(values, shares)]
    return [result.T.astype(BF16) for result in results]


def backward_units(units, share_grads, queries, keys, upstreams):
    shares = softmax_units(units)
    row_totals = [
        total_of([jnp.sum(p * g, axis=0, keepdims=True) for p, g in zip(parts, grads)])
        for parts, grads in zip(shares, share_grads)
    ]
    score_lows = [
        joined([p * (g - row_total) for p, g in zip(parts, grads)])
        for parts, grads, row_total in zip(shares, share_grads, row_totals)
    ]
    lows = [joined(parts) for parts in shares]
    query_grads = [dot(key, low, 0, 0).T * FACTOR for key, low in zip(keys, score_lows)]
    key_grads = [dot(low, query, 1, 0) for low, query in zip(score_lows, queries)]
    value_grads = [dot(low, upstream, 1, 0) for low, upstream in zip(lows, upstreams)]
    return query_grads, key_grads, value_grads


def causal_mask(block):
    return lax.broadcasted_iota(jnp.int32, (block, block), 0) <= lax.broadcasted_iota(
        jnp.int32, (block, block), 1
    )


def cut(scores, block):
    before = scores.shape[0] - block
    return [scores[:before], scores[before:]] if before else [scores]


def row_parts(key, query, block):
    parts = cut(dot(key, query, 1, 1), block)
    return parts[:-1] + [jnp.where(causal_mask(block), parts[-1], LOW)]


def head_span(h):
    return slice(h * DH, (h + 1) * DH)


def row_forward_kernel(q_ref, k_ref, v_ref, *refs):
    out_ref = refs[-1]
    steps, width = q_ref.shape
    block = min(BLOCK, steps)
    count = steps // block
    for first in range((count + 1) // 2):
        places = {first, count - 1 - first}
        units = [(i, head_span(h)) for i in sorted(places) for h in range(width // DH)]
        scores = [
            row_parts(
                k_ref[: (i + 1) * block, span], q_ref[i * block : (i + 1) * block, span], block
            )
            for i, span in units
        ]
        results = forward_units(scores, [v_ref[: (i + 1) * block, span] for i, span in units])
        for (i, span), result in zip(units, results):
            out_ref[i * block : (i + 1) * block, span] = result


def row_backward_kernel(q_ref, k_ref, v_ref, u_ref, dq_ref, dk_ref, dv_ref, dk_sum, dv_sum):
    steps = q_ref.shape[0]
    block = min(BLOCK, steps)
    count = steps // block
    order = range(count - 1, -1, -1)
    queries = [q_ref[i * block : (i + 1) * block, :] for i in order]
    upstreams = [u_ref[i * block : (i + 1) * block, :] for i in order]
    keys = [k_ref[: (i + 1) * block, :] for i in order]
    values = [v_ref[: (i + 1) * block, :] for i in order]
    scores = [row_parts(key, query, block) for key, query in zip(keys, queries)]
    share_grads = [
        cut(dot(value, upstream, 1, 1), block) for value, upstream in zip(values, upstreams)
    ]
    query_grads, key_grads, value_grads = backward_units(
        scores, share_grads, queries, keys, upstreams
    )
    for i, grad in zip(order, query_grads):
        dq_ref[i * block : (i + 1) * block, :] = grad.astype(BF16)
    for i, key_grad, value_grad in zip(order, key_grads, value_grads):
        rows = slice(0, (i + 1) * block)
        if i == count - 1:
            dk_sum[...] = key_grad
            dv_sum[...] = value_grad
        else:
            dk_sum[rows, :] += key_grad
            dv_sum[rows, :] += value_grad
    dk_ref[...] = (dk_sum[...] * FACTOR).astype(BF16)
    dv_ref[...] = dv_sum[...].astype(BF16)


def row_forward(queries, keys, values, *others):
    steps = queries.shape[0]
    head = pl.BlockSpec((steps, 2 * DH), lambda h: (0, h))
    return pl.pallas_call(
        row_forward_kernel,
        grid=(ROW_HEADS // 2,),
        in_specs=[head] * 3 + [pl.BlockSpec(memory_space=pl.ANY)] * len(others),
        out_specs=head,
        out_shape=jax.ShapeDtypeStruct((steps, ROW_WIDTH), BF16),
        compiler_params=params(),
        cost_estimate=cost("row_forward"),
        name="row_forward",
    )(queries, keys, values, *others)


def row_backward(queries, keys, values, upstream):
    steps = queries.shape[0]
    head = pl.BlockSpec((steps, DH), lambda h: (0, h))
    return pl.pallas_call(
        row_backward_kernel,
        grid=(ROW_HEADS,),
        in_specs=[head] * 4,
        out_specs=[head] * 3,
        out_shape=[jax.ShapeDtypeStruct(queries.shape, BF16)] * 3,
        scratch_shapes=[pltpu.VMEM((steps, DH), F32)] * 2,
        compiler_params=params(),
        cost_estimate=cost("row_backward"),
        name="row_backward",
    )(queries, keys, values, upstream)


def pack_kernel(q_ref, k_ref, v_ref, out_ref):
    group, _, cols, width = out_ref.shape
    for n, ref in enumerate((q_ref, k_ref, v_ref)):
        out_ref[:, n] = ref[...].reshape(group, cols, width)


def pack_specs(peers, cols):
    group = peers // 2
    return (
        pl.BlockSpec((group * cols, COL_WIDTH), lambda j: (j, ROW_WIDTH // COL_WIDTH)),
        pl.BlockSpec((group, 3, cols, COL_WIDTH), lambda j: (j, 0, 0, 0)),
    )


def pack(queries, keys, values, peers):
    cols = queries.shape[0] // peers
    apart, together = pack_specs(peers, cols)
    return pl.pallas_call(
        pack_kernel,
        grid=(2,),
        in_specs=[apart] * 3,
        out_specs=together,
        out_shape=jax.ShapeDtypeStruct((peers, 3, cols, COL_WIDTH), BF16),
        compiler_params=params(),
        cost_estimate=cost("pack"),
        name="pack",
    )(queries, keys, values)


def unpack_kernel(in_ref, _q, _k, _v, dq_ref, dk_ref, dv_ref):
    group = in_ref.shape[0] // pl.num_programs(0)
    peers = pl.ds(pl.program_id(0) * group, group)
    for n, ref in enumerate((dq_ref, dk_ref, dv_ref)):
        ref[...] = in_ref[peers, n].reshape(ref.shape)


def unpack(packed, dq, dk, dv):
    peers, _, cols, _ = packed.shape
    apart, _ = pack_specs(peers, cols)
    anywhere = pl.BlockSpec(memory_space=pl.ANY)
    return pl.pallas_call(
        unpack_kernel,
        grid=(2,),
        in_specs=[RESIDENT] + [anywhere] * 3,
        out_specs=[apart] * 3,
        out_shape=[jax.ShapeDtypeStruct(dq.shape, BF16)] * 3,
        input_output_aliases={1: 0, 2: 1, 3: 2},
        compiler_params=params(),
        cost_estimate=cost("unpack"),
        name="unpack",
    )(resident(packed), dq, dk, dv)


def column_mask(rows, cols):
    key = lax.broadcasted_iota(jnp.int32, (rows * cols, rows * cols), 0)
    query = lax.broadcasted_iota(jnp.int32, (rows * cols, rows * cols), 1)
    return (key <= query) & (key % cols == query % cols)


def head_tokens(ref, n, unit):
    cols, span = unit
    block = ref[:, cols, span] if n is None else ref[:, n, cols, span]
    return block.reshape(-1, DH)


def column_units(rows, width, span):
    together = max(1, 8 * 128**2 // (rows * span) ** 2)
    units = [
        (slice(c * span, (c + 1) * span), head_span(h))
        for c in range(width // span)
        for h in range(COL_HEADS)
    ]
    return [units[n : n + together] for n in range(0, len(units), together)]


def column_scores(in_ref, units, mask):
    return [
        [jnp.where(mask, dot(head_tokens(in_ref, 1, unit), head_tokens(in_ref, 0, unit), 1, 1), LOW)]
        for unit in units
    ]


def column_forward_kernel(in_ref, out_ref):
    rows, _, width, _ = in_ref.shape
    span = min(COLUMN_SPAN, width)
    mask = column_mask(rows, span)
    for units in column_units(rows, width, span):
        scores = column_scores(in_ref, units, mask)
        results = forward_units(scores, [head_tokens(in_ref, 2, unit) for unit in units])
        for (cols, lanes), result in zip(units, results):
            out_ref[:, cols, lanes] = result.reshape(rows, span, DH)


def column_backward_kernel(in_ref, u_ref, out_ref):
    rows, _, width, _ = in_ref.shape
    span = min(COLUMN_SPAN, width)
    mask = column_mask(rows, span)
    for units in column_units(rows, width, span):
        queries, keys, values = [
            [head_tokens(in_ref, n, unit) for unit in units] for n in range(3)
        ]
        upstreams = [head_tokens(u_ref, None, unit) for unit in units]
        scores = column_scores(in_ref, units, mask)
        share_grads = [[dot(v, u, 1, 1)] for v, u in zip(values, upstreams)]
        grads = backward_units(scores, share_grads, queries, keys, upstreams)
        for (cols, lanes), query_grad, key_grad, value_grad in zip(units, *grads):
            for n, grad in enumerate((query_grad, key_grad * FACTOR, value_grad)):
                out_ref[:, n, cols, lanes] = grad.astype(BF16).reshape(rows, span, DH)


def column_call(kernel, packed, upstream, name):
    rows, _, cols, width = packed.shape
    forward = upstream is None
    shape = (rows, cols, width) if forward else (rows, 3, cols, width)
    operands = (packed,) if forward else (packed, upstream)
    return pl.pallas_call(
        kernel,
        in_specs=[RESIDENT] * len(operands),
        out_specs=RESIDENT,
        out_shape=COLUMN_OUT(shape, BF16),
        compiler_params=params(),
        cost_estimate=cost(name),
        name=name,
    )(*map(resident, operands))


def upstream_kernel(place_ref, *refs):
    *w_refs, cot_ref, up_ref, full_ref = refs
    each, rows, _ = w_refs[0].shape

    @pl.when(pl.program_id(0) == 0)
    def _():
        for n, w_ref in enumerate(w_refs):
            for m in range(each):
                at = pl.multiple_of(place_ref[n * each + m], rows)
                full_ref[pl.ds(at, rows), :] = w_ref[m]

    up_ref[...] = dot(cot_ref[...], full_ref[...], 1, 1).astype(BF16)


def upstream_of(place, pieces, cotangent, name):
    steps, model = cotangent.shape
    each, rows, _ = pieces[0].shape
    width = each * len(pieces) * rows
    block = min(2 * BLOCK, steps)
    return pl.pallas_call(
        upstream_kernel,
        grid=(steps // block,),
        in_specs=[
            pl.BlockSpec(memory_space=pltpu.SMEM),
            *[whole(piece.shape) for piece in pieces],
            pl.BlockSpec((block, model), lambda t: (t, 0)),
        ],
        out_specs=[pl.BlockSpec((block, width), lambda t: (t, 0)), whole((width, model))],
        out_shape=[
            jax.ShapeDtypeStruct((steps, width), BF16),
            jax.ShapeDtypeStruct((width, model), BF16),
        ],
        compiler_params=params(),
        cost_estimate=cost(name),
        name=name,
    )(place, *pieces, cotangent)


def layer_kernel(row_ref, col_ref, w_row_ref, w_col_ref, out_ref):
    out_ref[...] = (
        dot(row_ref[...], w_row_ref[...], 1, 0) + dot(col_ref[...], w_col_ref[...], 1, 0)
    ).astype(BF16)


def layer_output(attn_row, attn_col, w_row, w_col):
    steps, width = attn_row.shape
    model = w_row.shape[1]
    block = min(BLOCK, steps)
    return pl.pallas_call(
        layer_kernel,
        grid=(steps // block,),
        in_specs=[pl.BlockSpec((block, width), lambda t: (t, 0))] * 2 + [whole(w_row.shape)] * 2,
        out_specs=pl.BlockSpec((block, model), lambda t: (t, 0)),
        out_shape=jax.ShapeDtypeStruct((steps, model), BF16),
        compiler_params=params(),
        cost_estimate=cost("layer_output"),
        name="layer_output",
    )(attn_row, attn_col, w_row, w_col)


def weight_kernel(factor, core_ref, attn_ref, cot_ref, keep_ref, send_ref):
    depths, pairs, rows, _ = keep_ref.shape
    product = dot(attn_ref[...], cot_ref[...], 0, 0) * factor
    first = core_ref[0] == 0
    for n in range(pairs):
        for z in range(depths):
            even, odd = [
                product[head * DH + z * rows : head * DH + (z + 1) * rows]
                for head in (2 * n, 2 * n + 1)
            ]
            keep_ref[z, n] = jnp.where(first, even, odd)
            send_ref[z, n] = jnp.where(first, odd, even).astype(send_ref.dtype)


def weight_parts(core, attn, cotangent, factor, depths, dtype, name):
    steps, width = attn.shape
    model = cotangent.shape[1]
    block = min(512, model)
    shape = (depths, width // DH // 2, DH // depths, model)
    out = pl.BlockSpec(shape[:-1] + (block,), lambda n: (0, 0, 0, n))
    return pl.pallas_call(
        functools.partial(weight_kernel, factor),
        grid=(model // block,),
        in_specs=[
            pl.BlockSpec(memory_space=pltpu.SMEM),
            whole((steps, width)),
            pl.BlockSpec((steps, block), lambda n: (0, n)),
        ],
        out_specs=[out, out],
        out_shape=[jax.ShapeDtypeStruct(shape, F32), jax.ShapeDtypeStruct(shape, dtype)],
        compiler_params=params(),
        cost_estimate=cost(name),
        name=name,
    )(core, attn, cotangent)


def flip(array, axis, bits, size):
    return lax.ppermute(array, axis, [(n, n ^ bits) for n in range(size)])


def after(member, *others):
    return lax.optimization_barrier((member, *others))[0]


def over_dp(pieces, dp_size):
    return [flip(piece, "dp", e, dp_size) for e, piece in enumerate(pieces, 1)]


def over_core(member, seq_size):
    return flip(member, "seq", 1, seq_size)


def over_plane(pieces, seq_size):
    return [flip(piece, "seq", 2 * d, seq_size) for d, piece in enumerate(pieces, 1)]


def gather_plane(shard, seq_size):
    pairs = seq_size // 2
    near = [shard, *over_plane([shard] * (pairs - 1), seq_size)]
    close, far = jnp.stack(near[: pairs // 2]), jnp.stack(near[pairs // 2 :])
    upper = lax.axis_index("seq") // 2 >= pairs // 2
    return jnp.where(upper, close, far), jnp.where(upper, far, close)


def piece_places(rows, seq_size, dp_size):
    me = lax.axis_index("seq")
    half = seq_size // 4
    c = (jnp.arange(2) ^ (me % 2))[:, None, None]
    z = (jnp.arange(dp_size) ^ lax.axis_index("dp"))[None, :, None]
    pair = (jnp.arange(half) ^ (me // 2 % half))[None, None, :]
    return (((pair * 2 + c) * dp_size + z) * rows).reshape(-1).astype(jnp.int32)


def cut_up(addends, me):
    def part(n):
        return functools.reduce(
            jnp.add,
            [lax.dynamic_index_in_dim(a, me ^ n, 0, False).astype(F32) for a in addends],
        )

    return part(0), [part(n).astype(BF16) for n in range(1, addends[0].shape[0])]


def sum_up(own, arrived):
    return functools.reduce(jnp.add, [member.astype(F32) for member in arrived], own)


def plane_kernel(pair_ref, *refs):
    *in_refs, own_ref, out_ref, total_ref = refs
    half, others = len(in_refs) // 2, out_ref.shape[0]
    for n in range(2):
        own, *arrived = in_refs[n * half : (n + 1) * half]
        rows = slice(n * own.shape[0], (n + 1) * own.shape[0])
        total_ref[rows] = sum_up(own[...], [ref[...] for ref in arrived])
    own_ref[...] = total_ref[pair_ref[0]]
    for d in range(others):
        out_ref[d] = total_ref[pair_ref[0] ^ (d + 1)].astype(BF16)


def plane_pieces(pair, row_own, row_sent, col_own, col_sent):
    operands = [row_own, *row_sent, col_own, *col_sent]
    pairs, rows, model = row_own.shape
    own, out = pl.pallas_call(
        plane_kernel,
        in_specs=[pl.BlockSpec(memory_space=pltpu.SMEM)] + [RESIDENT] * len(operands),
        out_specs=[RESIDENT] * 2,
        out_shape=[
            pltpu.VMEM((rows, model), F32),
            pltpu.VMEM((2 * pairs - 1, rows, model), BF16),
        ],
        scratch_shapes=[pltpu.VMEM((2 * pairs, rows, model), F32)],
        compiler_params=params(),
        cost_estimate=cost("plane_pieces"),
        name="plane_pieces",
    )(pair.reshape(1).astype(jnp.int32), *map(resident, operands))
    return own, [out[d] for d in range(out.shape[0])]


def body(queries, keys, values, out_weight, cotangent):
    seq_size, dp_size = lax.axis_size("seq"), lax.axis_size("dp")
    shape, cot_shape = queries.shape, cotangent.shape
    queries, keys, values, cotangent = [
        member.reshape(-1, member.shape[-1]) for member in (queries, keys, values, cotangent)
    ]
    steps = queries.shape[0]
    model = cotangent.shape[1]
    rows = out_weight.shape[0]
    factor = 1.0 / math.sqrt(steps * seq_size * dp_size)
    core = (lax.axis_index("seq") % 2).reshape(1).astype(jnp.int32)
    staged = seq_size == ROW_HEADS + COL_HEADS and rows % 16 == 0

    def exchange(member):
        return lax.all_to_all(member, "seq", split_axis=0, concat_axis=0, tiled=True)

    def weights(attn, name):
        return weight_parts(core, attn, cotangent, factor, dp_size, BF16, name)

    packed = pack(queries, keys, values, seq_size)
    arrived = exchange(packed)
    if staged:
        pair, depth = lax.axis_index("seq") // 2, lax.axis_index("dp")
        place = piece_places(rows, seq_size, dp_size)
        col_mine, row_mine = gather_plane(out_weight, seq_size)
        col_depth = [col_mine, *over_dp([col_mine] * (dp_size - 1), dp_size)]
        attn_row = row_forward(queries, keys, values, packed, col_mine)
        row_keep, row_send = weights(attn_row, "weight_row")
        col_depth = [after(member, row_keep) for member in col_depth]
        col_pieces = col_depth + [over_core(member, seq_size) for member in col_depth]
        row_received = over_core(after(row_send, *col_pieces), seq_size)
        row_mine = after(row_mine, *col_depth)
        row_depth = [row_mine, *over_dp([row_mine] * (dp_size - 1), dp_size)]
        arrived = after(arrived, row_keep)
        then = [row_depth[1]]
    else:
        place = jnp.zeros((1,), jnp.int32)
        full = lax.all_gather(out_weight, ("seq", "dp"), axis=0, tiled=True)
        row_pieces, col_pieces = [full[None, :ROW_WIDTH]], [full[None, ROW_WIDTH:]]
        attn_row = row_forward(queries, keys, values)
        then = []

    out_col = column_call(column_forward_kernel, arrived, None, "column_forward")
    attn_col = exchange(out_col).reshape(steps, COL_WIDTH)
    up_col, w_col = upstream_of(
        place, col_pieces, after(cotangent, out_col, *then), "upstream_col"
    )
    then = []
    if staged:
        row_own, row_out = cut_up((row_keep, after(row_received, up_col)), depth)
        row_pieces = row_depth + [
            over_core(after(member, up_col), seq_size) for member in row_depth
        ]
        then = row_depth + row_out
    up_arrived = exchange(after(up_col, attn_col, *then).reshape(seq_size, -1, COL_WIDTH))
    then = []
    if staged:
        row_sent = over_dp([after(piece, *row_depth) for piece in row_out], dp_size)
        col_keep, col_send = weights(attn_col, "weight_col")
        col_received = over_core(col_send, seq_size)
        then = [col_keep, *row_pieces, *row_sent[:SENT_FIRST]]
    up_arrived = after(up_arrived, *then)
    grads_col = column_call(column_backward_kernel, arrived, up_arrived, "column_backward")
    if staged:
        grads_col = after(grads_col, col_received)
    grads_arrived = exchange(grads_col)
    then = [grads_col]
    if staged:
        col_own, col_out = cut_up((after(col_keep, grads_col), col_received), depth)
        col_sent = over_dp(col_out, dp_size)
        then = col_out
    up_row, w_row = upstream_of(place, row_pieces, after(cotangent, *then), "upstream_row")
    dq, dk, dv = row_backward(queries, keys, values, up_row)
    layer_out = layer_output(after(attn_row, dq), attn_col, w_row, w_col)
    if staged:
        own, out = plane_pieces(
            pair,
            row_own,
            row_sent,
            col_own,
            [after(member, layer_out) for member in col_sent],
        )
        sent = over_plane(out, seq_size)
        dq, dk, dv = unpack(after(grads_arrived, *out), dq, dk, dv)
        weight_grad = sum_up(own, [after(member, dq) for member in sent])
    else:
        local = []
        for member, name in ((attn_row, "weight_row"), (attn_col, "weight_col")):
            even, odd = weight_parts(
                jnp.zeros((1,), jnp.int32), member, cotangent, factor, 1, F32, name
            )
            local.append(jnp.stack([even[0], odd[0]], axis=1).reshape(-1, model))
        weight_grad = lax.psum_scatter(
            jnp.concatenate(local), ("seq", "dp"), scatter_dimension=0, tiled=True
        )
        dq, dk, dv = unpack(grads_arrived, dq, dk, dv)
    return (
        layer_out.reshape(cot_shape),
        dq.reshape(shape),
        dk.reshape(shape),
        dv.reshape(shape),
        weight_grad,
    )


def solution(mesh):
    tokens = P("dp", "seq", None, None)
    weights = P(("seq", "dp"), None)
    return jax.shard_map(
        body,
        mesh=mesh,
        in_specs=(tokens, tokens, tokens, weights, tokens),
        out_specs=(tokens, tokens, tokens, tokens, weights),
        check_vma=False,
    )
```

```python
import functools
import math

import jax
import jax.numpy as jnp
from jax import lax
from jax.experimental import pallas as pl
from jax.experimental.pallas import tpu as pltpu
from jax.sharding import PartitionSpec as P

ROW_HEADS = 4
COL_HEADS = 4
DH = 128
ROW_WIDTH = ROW_HEADS * DH
COL_WIDTH = COL_HEADS * DH
FACTOR = 1.0 / math.sqrt(DH)
EXP_SCALE = FACTOR * math.log2(math.e)
BLOCK = 256
COLUMN_SPAN = 16
COLUMN_OUT = jax.ShapeDtypeStruct
SENT_FIRST = 2
LOW = -1e30
BF16 = jnp.bfloat16
F32 = jnp.float32
VMEM = 58 * 1024 * 1024
DECLARED = {
    "pack": 0.6, "unpack": 0.6, "row_forward": 100.0, "row_backward": 1.4, "column_forward": 110.0,
    "column_backward": 120.0, "upstream_col": 70.0, "upstream_row": 0.1, "weight_row": 0.6,
    "weight_col": 0.1, "layer_output": 0.9, "plane_pieces": 0.1,
}
DECLARED_FLOPS = 1.15e9


def cost(name):
    return pl.CostEstimate(
        flops=int(DECLARED[name] * DECLARED_FLOPS), transcendentals=0, bytes_accessed=0
    )


def params():
    return pltpu.CompilerParams(vmem_limit_bytes=VMEM)


def resident(array):
    return pltpu.with_memory_space_constraint(array, pltpu.VMEM)


RESIDENT = pl.BlockSpec(memory_space=pltpu.VMEM)


def dot(a, b, a_dim, b_dim):
    return lax.dot_general(a, b, (((a_dim,), (b_dim,)), ((), ())), preferred_element_type=F32)


def whole(shape):
    return pl.BlockSpec(shape, lambda *_: (0,) * len(shape))


def total_of(members):
    return functools.reduce(jnp.add, members)


def joined(parts):
    parts = [part.astype(BF16) for part in parts]
    return parts[0] if len(parts) == 1 else jnp.concatenate(parts, axis=0)


def softmax_units(units):
    peaks = [
        functools.reduce(jnp.maximum, [jnp.max(s, axis=0, keepdims=True) for s in parts])
        * EXP_SCALE
        for parts in units
    ]
    raised = [
        [jnp.exp2(s * EXP_SCALE - peak) for s in parts] for parts, peak in zip(units, peaks)
    ]
    inverses = [
        1.0 / total_of([jnp.sum(e, axis=0, keepdims=True) for e in parts]) for parts in raised
    ]
    return [[e * inverse for e in parts] for parts, inverse in zip(raised, inverses)]


def forward_units(units, values):
    shares = [joined(parts) for parts in softmax_units(units)]
    results = [dot(value, share, 0, 0) for value, share in zip(values, shares)]
    return [result.T.astype(BF16) for result in results]


def backward_units(units, share_grads, queries, keys, upstreams):
    shares = softmax_units(units)
    row_totals = [
        total_of([jnp.sum(p * g, axis=0, keepdims=True) for p, g in zip(parts, grads)])
        for parts, grads in zip(shares, share_grads)
    ]
    score_lows = [
        joined([p * (g - row_total) for p, g in zip(parts, grads)])
        for parts, grads, row_total in zip(shares, share_grads, row_totals)
    ]
    lows = [joined(parts) for parts in shares]
    query_grads = [dot(key, low, 0, 0).T * FACTOR for key, low in zip(keys, score_lows)]
    key_grads = [dot(low, query, 1, 0) for low, query in zip(score_lows, queries)]
    value_grads = [dot(low, upstream, 1, 0) for low, upstream in zip(lows, upstreams)]
    return query_grads, key_grads, value_grads


def causal_mask(block):
    return lax.broadcasted_iota(jnp.int32, (block, block), 0) <= lax.broadcasted_iota(
        jnp.int32, (block, block), 1
    )


def cut(scores, block):
    before = scores.shape[0] - block
    return [scores[:before], scores[before:]] if before else [scores]


def row_parts(key, query, block):
    parts = cut(dot(key, query, 1, 1), block)
    return parts[:-1] + [jnp.where(causal_mask(block), parts[-1], LOW)]


def head_span(h):
    return slice(h * DH, (h + 1) * DH)


def row_forward_kernel(q_ref, k_ref, v_ref, *refs):
    out_ref = refs[-1]
    steps, width = q_ref.shape
    block = min(BLOCK, steps)
    count = steps // block
    for first in range((count + 1) // 2):
        places = {first, count - 1 - first}
        units = [(i, head_span(h)) for i in sorted(places) for h in range(width // DH)]
        scores = [
            row_parts(
                k_ref[: (i + 1) * block, span], q_ref[i * block : (i + 1) * block, span], block
            )
            for i, span in units
        ]
        results = forward_units(scores, [v_ref[: (i + 1) * block, span] for i, span in units])
        for (i, span), result in zip(units, results):
            out_ref[i * block : (i + 1) * block, span] = result


def row_backward_kernel(q_ref, k_ref, v_ref, u_ref, dq_ref, dk_ref, dv_ref, dk_sum, dv_sum):
    steps = q_ref.shape[0]
    block = min(BLOCK, steps)
    count = steps // block
    order = range(count - 1, -1, -1)
    queries = [q_ref[i * block : (i + 1) * block, :] for i in order]
    upstreams = [u_ref[i * block : (i + 1) * block, :] for i in order]
    keys = [k_ref[: (i + 1) * block, :] for i in order]
    values = [v_ref[: (i + 1) * block, :] for i in order]
    scores = [row_parts(key, query, block) for key, query in zip(keys, queries)]
    share_grads = [
        cut(dot(value, upstream, 1, 1), block) for value, upstream in zip(values, upstreams)
    ]
    query_grads, key_grads, value_grads = backward_units(
        scores, share_grads, queries, keys, upstreams
    )
    for i, grad in zip(order, query_grads):
        dq_ref[i * block : (i + 1) * block, :] = grad.astype(BF16)
    for i, key_grad, value_grad in zip(order, key_grads, value_grads):
        rows = slice(0, (i + 1) * block)
        if i == count - 1:
            dk_sum[...] = key_grad
            dv_sum[...] = value_grad
        else:
            dk_sum[rows, :] += key_grad
            dv_sum[rows, :] += value_grad
    dk_ref[...] = (dk_sum[...] * FACTOR).astype(BF16)
    dv_ref[...] = dv_sum[...].astype(BF16)


def row_forward(queries, keys, values, *others):
    steps = queries.shape[0]
    head = pl.BlockSpec((steps, 2 * DH), lambda h: (0, h))
    return pl.pallas_call(
        row_forward_kernel,
        grid=(ROW_HEADS // 2,),
        in_specs=[head] * 3 + [pl.BlockSpec(memory_space=pl.ANY)] * len(others),
        out_specs=head,
        out_shape=jax.ShapeDtypeStruct((steps, ROW_WIDTH), BF16),
        compiler_params=params(),
        cost_estimate=cost("row_forward"),
        name="row_forward",
    )(queries, keys, values, *others)


def row_backward(queries, keys, values, upstream):
    steps = queries.shape[0]
    head = pl.BlockSpec((steps, DH), lambda h: (0, h))
    return pl.pallas_call(
        row_backward_kernel,
        grid=(ROW_HEADS,),
        in_specs=[head] * 4,
        out_specs=[head] * 3,
        out_shape=[jax.ShapeDtypeStruct(queries.shape, BF16)] * 3,
        scratch_shapes=[pltpu.VMEM((steps, DH), F32)] * 2,
        compiler_params=params(),
        cost_estimate=cost("row_backward"),
        name="row_backward",
    )(queries, keys, values, upstream)


def pack_kernel(q_ref, k_ref, v_ref, out_ref):
    group, _, cols, width = out_ref.shape
    for n, ref in enumerate((q_ref, k_ref, v_ref)):
        out_ref[:, n] = ref[...].reshape(group, cols, width)


def pack_specs(peers, cols):
    group = peers // 2
    return (
        pl.BlockSpec((group * cols, COL_WIDTH), lambda j: (j, ROW_WIDTH // COL_WIDTH)),
        pl.BlockSpec((group, 3, cols, COL_WIDTH), lambda j: (j, 0, 0, 0)),
    )


def pack(queries, keys, values, peers):
    cols = queries.shape[0] // peers
    apart, together = pack_specs(peers, cols)
    return pl.pallas_call(
        pack_kernel,
        grid=(2,),
        in_specs=[apart] * 3,
        out_specs=together,
        out_shape=jax.ShapeDtypeStruct((peers, 3, cols, COL_WIDTH), BF16),
        compiler_params=params(),
        cost_estimate=cost("pack"),
        name="pack",
    )(queries, keys, values)


def unpack_kernel(in_ref, _q, _k, _v, dq_ref, dk_ref, dv_ref):
    group = in_ref.shape[0] // pl.num_programs(0)
    peers = pl.ds(pl.program_id(0) * group, group)
    for n, ref in enumerate((dq_ref, dk_ref, dv_ref)):
        ref[...] = in_ref[peers, n].reshape(ref.shape)


def unpack(packed, dq, dk, dv):
    peers, _, cols, _ = packed.shape
    apart, _ = pack_specs(peers, cols)
    anywhere = pl.BlockSpec(memory_space=pl.ANY)
    return pl.pallas_call(
        unpack_kernel,
        grid=(2,),
        in_specs=[RESIDENT] + [anywhere] * 3,
        out_specs=[apart] * 3,
        out_shape=[jax.ShapeDtypeStruct(dq.shape, BF16)] * 3,
        input_output_aliases={1: 0, 2: 1, 3: 2},
        compiler_params=params(),
        cost_estimate=cost("unpack"),
        name="unpack",
    )(resident(packed), dq, dk, dv)


def column_mask(rows, cols):
    key = lax.broadcasted_iota(jnp.int32, (rows * cols, rows * cols), 0)
    query = lax.broadcasted_iota(jnp.int32, (rows * cols, rows * cols), 1)
    return (key <= query) & (key % cols == query % cols)


def head_tokens(ref, n, unit):
    cols, span = unit
    block = ref[:, cols, span] if n is None else ref[:, n, cols, span]
    return block.reshape(-1, DH)


def column_units(rows, width, span):
    together = max(1, 8 * 128**2 // (rows * span) ** 2)
    units = [
        (slice(c * span, (c + 1) * span), head_span(h))
        for c in range(width // span)
        for h in range(COL_HEADS)
    ]
    return [units[n : n + together] for n in range(0, len(units), together)]


def column_scores(in_ref, units, mask):
    return [
        [jnp.where(mask, dot(head_tokens(in_ref, 1, unit), head_tokens(in_ref, 0, unit), 1, 1), LOW)]
        for unit in units
    ]


def column_forward_kernel(in_ref, out_ref):
    rows, _, width, _ = in_ref.shape
    span = min(COLUMN_SPAN, width)
    mask = column_mask(rows, span)
    for units in column_units(rows, width, span):
        scores = column_scores(in_ref, units, mask)
        results = forward_units(scores, [head_tokens(in_ref, 2, unit) for unit in units])
        for (cols, lanes), result in zip(units, results):
            out_ref[:, cols, lanes] = result.reshape(rows, span, DH)


def column_backward_kernel(in_ref, u_ref, out_ref):
    rows, _, width, _ = in_ref.shape
    span = min(COLUMN_SPAN, width)
    mask = column_mask(rows, span)
    for units in column_units(rows, width, span):
        queries, keys, values = [
            [head_tokens(in_ref, n, unit) for unit in units] for n in range(3)
        ]
        upstreams = [head_tokens(u_ref, None, unit) for unit in units]
        scores = column_scores(in_ref, units, mask)
        share_grads = [[dot(v, u, 1, 1)] for v, u in zip(values, upstreams)]
        grads = backward_units(scores, share_grads, queries, keys, upstreams)
        for (cols, lanes), query_grad, key_grad, value_grad in zip(units, *grads):
            for n, grad in enumerate((query_grad, key_grad * FACTOR, value_grad)):
                out_ref[:, n, cols, lanes] = grad.astype(BF16).reshape(rows, span, DH)


def column_call(kernel, packed, upstream, name):
    rows, _, cols, width = packed.shape
    forward = upstream is None
    shape = (rows, cols, width) if forward else (rows, 3, cols, width)
    operands = (packed,) if forward else (packed, upstream)
    return pl.pallas_call(
        kernel,
        in_specs=[RESIDENT] * len(operands),
        out_specs=RESIDENT,
        out_shape=COLUMN_OUT(shape, BF16),
        compiler_params=params(),
        cost_estimate=cost(name),
        name=name,
    )(*map(resident, operands))


def upstream_kernel(place_ref, *refs):
    *w_refs, cot_ref, up_ref, full_ref = refs
    each, rows, _ = w_refs[0].shape

    @pl.when(pl.program_id(0) == 0)
    def _():
        for n, w_ref in enumerate(w_refs):
            for m in range(each):
                at = pl.multiple_of(place_ref[n * each + m], rows)
                full_ref[pl.ds(at, rows), :] = w_ref[m]

    up_ref[...] = dot(cot_ref[...], full_ref[...], 1, 1).astype(BF16)


def upstream_of(place, pieces, cotangent, name):
    steps, model = cotangent.shape
    each, rows, _ = pieces[0].shape
    width = each * len(pieces) * rows
    block = min(2 * BLOCK, steps)
    return pl.pallas_call(
        upstream_kernel,
        grid=(steps // block,),
        in_specs=[
            pl.BlockSpec(memory_space=pltpu.SMEM),
            *[whole(piece.shape) for piece in pieces],
            pl.BlockSpec((block, model), lambda t: (t, 0)),
        ],
        out_specs=[pl.BlockSpec((block, width), lambda t: (t, 0)), whole((width, model))],
        out_shape=[
            jax.ShapeDtypeStruct((steps, width), BF16),
            jax.ShapeDtypeStruct((width, model), BF16),
        ],
        compiler_params=params(),
        cost_estimate=cost(name),
        name=name,
    )(place, *pieces, cotangent)


def layer_kernel(row_ref, col_ref, w_row_ref, w_col_ref, out_ref):
    out_ref[...] = (
        dot(row_ref[...], w_row_ref[...], 1, 0) + dot(col_ref[...], w_col_ref[...], 1, 0)
    ).astype(BF16)


def layer_output(attn_row, attn_col, w_row, w_col):
    steps, width = attn_row.shape
    model = w_row.shape[1]
    block = min(BLOCK, steps)
    return pl.pallas_call(
        layer_kernel,
        grid=(steps // block,),
        in_specs=[pl.BlockSpec((block, width), lambda t: (t, 0))] * 2 + [whole(w_row.shape)] * 2,
        out_specs=pl.BlockSpec((block, model), lambda t: (t, 0)),
        out_shape=jax.ShapeDtypeStruct((steps, model), BF16),
        compiler_params=params(),
        cost_estimate=cost("layer_output"),
        name="layer_output",
    )(attn_row, attn_col, w_row, w_col)


def weight_kernel(factor, core_ref, attn_ref, cot_ref, keep_ref, send_ref):
    depths, pairs, rows, _ = keep_ref.shape
    product = dot(attn_ref[...], cot_ref[...], 0, 0) * factor
    first = core_ref[0] == 0
    for n in range(pairs):
        for z in range(depths):
            even, odd = [
                product[head * DH + z * rows : head * DH + (z + 1) * rows]
                for head in (2 * n, 2 * n + 1)
            ]
            keep_ref[z, n] = jnp.where(first, even, odd)
            send_ref[z, n] = jnp.where(first, odd, even).astype(send_ref.dtype)


def weight_parts(core, attn, cotangent, factor, depths, dtype, name):
    steps, width = attn.shape
    model = cotangent.shape[1]
    block = min(512, model)
    shape = (depths, width // DH // 2, DH // depths, model)
    out = pl.BlockSpec(shape[:-1] + (block,), lambda n: (0, 0, 0, n))
    return pl.pallas_call(
        functools.partial(weight_kernel, factor),
        grid=(model // block,),
        in_specs=[
            pl.BlockSpec(memory_space=pltpu.SMEM),
            whole((steps, width)),
            pl.BlockSpec((steps, block), lambda n: (0, n)),
        ],
        out_specs=[out, out],
        out_shape=[jax.ShapeDtypeStruct(shape, F32), jax.ShapeDtypeStruct(shape, dtype)],
        compiler_params=params(),
        cost_estimate=cost(name),
        name=name,
    )(core, attn, cotangent)


def flip(array, axis, bits, size):
    return lax.ppermute(array, axis, [(n, n ^ bits) for n in range(size)])


def after(member, *others):
    return lax.optimization_barrier((member, *others))[0]


def over_dp(pieces, dp_size):
    return [flip(piece, "dp", e, dp_size) for e, piece in enumerate(pieces, 1)]


def over_core(member, seq_size):
    return flip(member, "seq", 1, seq_size)


def over_plane(pieces, seq_size):
    return [flip(piece, "seq", 2 * d, seq_size) for d, piece in enumerate(pieces, 1)]


def gather_plane(shard, seq_size):
    pairs = seq_size // 2
    near = [shard, *over_plane([shard] * (pairs - 1), seq_size)]
    close, far = jnp.stack(near[: pairs // 2]), jnp.stack(near[pairs // 2 :])
    upper = lax.axis_index("seq") // 2 >= pairs // 2
    return jnp.where(upper, close, far), jnp.where(upper, far, close)


def piece_places(rows, seq_size, dp_size):
    me = lax.axis_index("seq")
    half = seq_size // 4
    c = (jnp.arange(2) ^ (me % 2))[:, None, None]
    z = (jnp.arange(dp_size) ^ lax.axis_index("dp"))[None, :, None]
    pair = (jnp.arange(half) ^ (me // 2 % half))[None, None, :]
    return (((pair * 2 + c) * dp_size + z) * rows).reshape(-1).astype(jnp.int32)


def cut_up(addends, me):
    def part(n):
        return functools.reduce(
            jnp.add,
            [lax.dynamic_index_in_dim(a, me ^ n, 0, False).astype(F32) for a in addends],
        )

    return part(0), [part(n).astype(BF16) for n in range(1, addends[0].shape[0])]


def sum_up(own, arrived):
    return functools.reduce(jnp.add, [member.astype(F32) for member in arrived], own)


def plane_kernel(pair_ref, *refs):
    *in_refs, own_ref, out_ref, total_ref = refs
    half, others = len(in_refs) // 2, out_ref.shape[0]
    for n in range(2):
        own, *arrived = in_refs[n * half : (n + 1) * half]
        rows = slice(n * own.shape[0], (n + 1) * own.shape[0])
        total_ref[rows] = sum_up(own[...], [ref[...] for ref in arrived])
    own_ref[...] = total_ref[pair_ref[0]]
    for d in range(others):
        out_ref[d] = total_ref[pair_ref[0] ^ (d + 1)].astype(BF16)


def plane_pieces(pair, row_own, row_sent, col_own, col_sent):
    operands = [row_own, *row_sent, col_own, *col_sent]
    pairs, rows, model = row_own.shape
    own, out = pl.pallas_call(
        plane_kernel,
        in_specs=[pl.BlockSpec(memory_space=pltpu.SMEM)] + [RESIDENT] * len(operands),
        out_specs=[RESIDENT] * 2,
        out_shape=[
            pltpu.VMEM((rows, model), F32),
            pltpu.VMEM((2 * pairs - 1, rows, model), BF16),
        ],
        scratch_shapes=[pltpu.VMEM((2 * pairs, rows, model), F32)],
        compiler_params=params(),
        cost_estimate=cost("plane_pieces"),
        name="plane_pieces",
    )(pair.reshape(1).astype(jnp.int32), *map(resident, operands))
    return own, [out[d] for d in range(out.shape[0])]


def body(queries, keys, values, out_weight, cotangent):
    seq_size, dp_size = lax.axis_size("seq"), lax.axis_size("dp")
    shape, cot_shape = queries.shape, cotangent.shape
    queries, keys, values, cotangent = [
        member.reshape(-1, member.shape[-1]) for member in (queries, keys, values, cotangent)
    ]
    steps = queries.shape[0]
    model = cotangent.shape[1]
    rows = out_weight.shape[0]
    factor = 1.0 / math.sqrt(steps * seq_size * dp_size)
    core = (lax.axis_index("seq") % 2).reshape(1).astype(jnp.int32)
    staged = seq_size == ROW_HEADS + COL_HEADS and rows % 16 == 0

    def exchange(member):
        return lax.all_to_all(member, "seq", split_axis=0, concat_axis=0, tiled=True)

    def weights(attn, name):
        return weight_parts(core, attn, cotangent, factor, dp_size, BF16, name)

    packed = pack(queries, keys, values, seq_size)
    arrived = exchange(packed)
    if staged:
        pair, depth = lax.axis_index("seq") // 2, lax.axis_index("dp")
        place = piece_places(rows, seq_size, dp_size)
        col_mine, row_mine = gather_plane(out_weight, seq_size)
        col_depth = [col_mine, *over_dp([col_mine] * (dp_size - 1), dp_size)]
        attn_row = row_forward(queries, keys, values, packed, col_mine)
        row_keep, row_send = weights(attn_row, "weight_row")
        col_depth = [after(member, row_keep) for member in col_depth]
        col_pieces = col_depth + [over_core(member, seq_size) for member in col_depth]
        row_received = over_core(after(row_send, *col_pieces), seq_size)
        row_mine = after(row_mine, *col_depth)
        row_depth = [row_mine, *over_dp([row_mine] * (dp_size - 1), dp_size)]
        arrived = after(arrived, row_keep)
        then = [row_depth[1]]
    else:
        place = jnp.zeros((1,), jnp.int32)
        full = lax.all_gather(out_weight, ("seq", "dp"), axis=0, tiled=True)
        row_pieces, col_pieces = [full[None, :ROW_WIDTH]], [full[None, ROW_WIDTH:]]
        attn_row = row_forward(queries, keys, values)
        then = []

    out_col = column_call(column_forward_kernel, arrived, None, "column_forward")
    attn_col = exchange(out_col).reshape(steps, COL_WIDTH)
    up_col, w_col = upstream_of(
        place, col_pieces, after(cotangent, out_col, *then), "upstream_col"
    )
    then = []
    if staged:
        row_own, row_out = cut_up((row_keep, after(row_received, up_col)), depth)
        row_pieces = row_depth + [
            over_core(after(member, up_col), seq_size) for member in row_depth
        ]
        then = row_depth + row_out
    up_arrived = exchange(after(up_col, attn_col, *then).reshape(seq_size, -1, COL_WIDTH))
    then = []
    if staged:
        row_sent = over_dp([after(piece, *row_depth) for piece in row_out], dp_size)
        col_keep, col_send = weights(attn_col, "weight_col")
        col_received = over_core(col_send, seq_size)
        then = [col_keep, *row_pieces, *row_sent[:SENT_FIRST]]
    up_arrived = after(up_arrived, *then)
    grads_col = column_call(column_backward_kernel, arrived, up_arrived, "column_backward")
    if staged:
        grads_col = after(grads_col, col_received)
    grads_arrived = exchange(grads_col)
    then = [grads_col]
    if staged:
        col_own, col_out = cut_up((after(col_keep, grads_col), col_received), depth)
        col_sent = over_dp(col_out, dp_size)
        then = col_out
    up_row, w_row = upstream_of(place, row_pieces, after(cotangent, *then), "upstream_row")
    dq, dk, dv = row_backward(queries, keys, values, up_row)
    layer_out = layer_output(after(attn_row, dq), attn_col, w_row, w_col)
    if staged:
        own, out = plane_pieces(
            pair,
            row_own,
            row_sent,
            col_own,
            [after(member, layer_out) for member in col_sent],
        )
        sent = over_plane(out, seq_size)
        dq, dk, dv = unpack(after(grads_arrived, *out), dq, dk, dv)
        weight_grad = sum_up(own, [after(member, dq) for member in sent])
    else:
        local = []
        for member, name in ((attn_row, "weight_row"), (attn_col, "weight_col")):
            even, odd = weight_parts(
                jnp.zeros((1,), jnp.int32), member, cotangent, factor, 1, F32, name
            )
            local.append(jnp.stack([even[0], odd[0]], axis=1).reshape(-1, model))
        weight_grad = lax.psum_scatter(
            jnp.concatenate(local), ("seq", "dp"), scatter_dimension=0, tiled=True
        )
        dq, dk, dv = unpack(grads_arrived, dq, dk, dv)
    return (
        layer_out.reshape(cot_shape),
        dq.reshape(shape),
        dk.reshape(shape),
        dv.reshape(shape),
        weight_grad,
    )


def solution(mesh):
    tokens = P("dp", "seq", None, None)
    weights = P(("seq", "dp"), None)
    return jax.shard_map(
        body,
        mesh=mesh,
        in_specs=(tokens, tokens, tokens, weights, tokens),
        out_specs=(tokens, tokens, tokens, tokens, weights),
        check_vma=False,
    )
```

```python
import functools
import math

import jax
import jax.numpy as jnp
from jax import lax
from jax.experimental import pallas as pl
from jax.experimental.pallas import tpu as pltpu
from jax.sharding import PartitionSpec as P

ROW_HEADS = 4
COL_HEADS = 4
DH = 128
ROW_WIDTH = ROW_HEADS * DH
COL_WIDTH = COL_HEADS * DH
FACTOR = 1.0 / math.sqrt(DH)
EXP_SCALE = FACTOR * math.log2(math.e)
BLOCK = 256
COLUMN_SPAN = 16
COLUMN_OUT = jax.ShapeDtypeStruct
SENT_FIRST = 2
LOW = -1e30
BF16 = jnp.bfloat16
F32 = jnp.float32
VMEM = 58 * 1024 * 1024
DECLARED = {
    "pack": 0.6, "unpack": 0.6, "row_forward": 100.0, "row_backward": 1.4, "column_forward": 110.0,
    "column_backward": 120.0, "upstream_col": 70.0, "upstream_row": 0.1, "weight_row": 0.6,
    "weight_col": 0.1, "layer_output": 0.9, "plane_pieces": 0.1,
}
DECLARED_FLOPS = 1.15e9


def cost(name):
    return pl.CostEstimate(
        flops=int(DECLARED[name] * DECLARED_FLOPS), transcendentals=0, bytes_accessed=0
    )


def params():
    return pltpu.CompilerParams(vmem_limit_bytes=VMEM)


def resident(array):
    return pltpu.with_memory_space_constraint(array, pltpu.VMEM)


RESIDENT = pl.BlockSpec(memory_space=pltpu.VMEM)


def dot(a, b, a_dim, b_dim):
    return lax.dot_general(a, b, (((a_dim,), (b_dim,)), ((), ())), preferred_element_type=F32)


def whole(shape):
    return pl.BlockSpec(shape, lambda *_: (0,) * len(shape))


def total_of(members):
    return functools.reduce(jnp.add, members)


def joined(parts):
    parts = [part.astype(BF16) for part in parts]
    return parts[0] if len(parts) == 1 else jnp.concatenate(parts, axis=0)


def softmax_units(units):
    peaks = [
        functools.reduce(jnp.maximum, [jnp.max(s, axis=0, keepdims=True) for s in parts])
        * EXP_SCALE
        for parts in units
    ]
    raised = [
        [jnp.exp2(s * EXP_SCALE - peak) for s in parts] for parts, peak in zip(units, peaks)
    ]
    inverses = [
        1.0 / total_of([jnp.sum(e, axis=0, keepdims=True) for e in parts]) for parts in raised
    ]
    return [[e * inverse for e in parts] for parts, inverse in zip(raised, inverses)]


def forward_units(units, values):
    shares = [joined(parts) for parts in softmax_units(units)]
    results = [dot(value, share, 0, 0) for value, share in zip(values, shares)]
    return [result.T.astype(BF16) for result in results]


def backward_units(units, share_grads, queries, keys, upstreams):
    shares = softmax_units(units)
    row_totals = [
        total_of([jnp.sum(p * g, axis=0, keepdims=True) for p, g in zip(parts, grads)])
        for parts, grads in zip(shares, share_grads)
    ]
    score_lows = [
        joined([p * (g - row_total) for p, g in zip(parts, grads)])
        for parts, grads, row_total in zip(shares, share_grads, row_totals)
    ]
    lows = [joined(parts) for parts in shares]
    query_grads = [dot(key, low, 0, 0).T * FACTOR for key, low in zip(keys, score_lows)]
    key_grads = [dot(low, query, 1, 0) for low, query in zip(score_lows, queries)]
    value_grads = [dot(low, upstream, 1, 0) for low, upstream in zip(lows, upstreams)]
    return query_grads, key_grads, value_grads


def causal_mask(block):
    return lax.broadcasted_iota(jnp.int32, (block, block), 0) <= lax.broadcasted_iota(
        jnp.int32, (block, block), 1
    )


def cut(scores, block):
    before = scores.shape[0] - block
    return [scores[:before], scores[before:]] if before else [scores]


def row_parts(key, query, block):
    parts = cut(dot(key, query, 1, 1), block)
    return parts[:-1] + [jnp.where(causal_mask(block), parts[-1], LOW)]


def head_span(h):
    return slice(h * DH, (h + 1) * DH)


def row_forward_kernel(q_ref, k_ref, v_ref, *refs):
    out_ref = refs[-1]
    steps, width = q_ref.shape
    block = min(BLOCK, steps)
    count = steps // block
    for first in range((count + 1) // 2):
        places = {first, count - 1 - first}
        units = [(i, head_span(h)) for i in sorted(places) for h in range(width // DH)]
        scores = [
            row_parts(
                k_ref[: (i + 1) * block, span], q_ref[i * block : (i + 1) * block, span], block
            )
            for i, span in units
        ]
        results = forward_units(scores, [v_ref[: (i + 1) * block, span] for i, span in units])
        for (i, span), result in zip(units, results):
            out_ref[i * block : (i + 1) * block, span] = result


def row_backward_kernel(q_ref, k_ref, v_ref, u_ref, dq_ref, dk_ref, dv_ref, dk_sum, dv_sum):
    steps = q_ref.shape[0]
    block = min(BLOCK, steps)
    count = steps // block
    order = range(count - 1, -1, -1)
    queries = [q_ref[i * block : (i + 1) * block, :] for i in order]
    upstreams = [u_ref[i * block : (i + 1) * block, :] for i in order]
    keys = [k_ref[: (i + 1) * block, :] for i in order]
    values = [v_ref[: (i + 1) * block, :] for i in order]
    scores = [row_parts(key, query, block) for key, query in zip(keys, queries)]
    share_grads = [
        cut(dot(value, upstream, 1, 1), block) for value, upstream in zip(values, upstreams)
    ]
    query_grads, key_grads, value_grads = backward_units(
        scores, share_grads, queries, keys, upstreams
    )
    for i, grad in zip(order, query_grads):
        dq_ref[i * block : (i + 1) * block, :] = grad.astype(BF16)
    for i, key_grad, value_grad in zip(order, key_grads, value_grads):
        rows = slice(0, (i + 1) * block)
        if i == count - 1:
            dk_sum[...] = key_grad
            dv_sum[...] = value_grad
        else:
            dk_sum[rows, :] += key_grad
            dv_sum[rows, :] += value_grad
    dk_ref[...] = (dk_sum[...] * FACTOR).astype(BF16)
    dv_ref[...] = dv_sum[...].astype(BF16)


def row_forward(queries, keys, values, *others):
    steps = queries.shape[0]
    head = pl.BlockSpec((steps, 2 * DH), lambda h: (0, h))
    return pl.pallas_call(
        row_forward_kernel,
        grid=(ROW_HEADS // 2,),
        in_specs=[head] * 3 + [pl.BlockSpec(memory_space=pl.ANY)] * len(others),
        out_specs=head,
        out_shape=jax.ShapeDtypeStruct((steps, ROW_WIDTH), BF16),
        compiler_params=params(),
        cost_estimate=cost("row_forward"),
        name="row_forward",
    )(queries, keys, values, *others)


def row_backward(queries, keys, values, upstream):
    steps = queries.shape[0]
    head = pl.BlockSpec((steps, DH), lambda h: (0, h))
    return pl.pallas_call(
        row_backward_kernel,
        grid=(ROW_HEADS,),
        in_specs=[head] * 4,
        out_specs=[head] * 3,
        out_shape=[jax.ShapeDtypeStruct(queries.shape, BF16)] * 3,
        scratch_shapes=[pltpu.VMEM((steps, DH), F32)] * 2,
        compiler_params=params(),
        cost_estimate=cost("row_backward"),
        name="row_backward",
    )(queries, keys, values, upstream)


def pack_kernel(q_ref, k_ref, v_ref, out_ref):
    group, _, cols, width = out_ref.shape
    for n, ref in enumerate((q_ref, k_ref, v_ref)):
        out_ref[:, n] = ref[...].reshape(group, cols, width)


def pack_specs(peers, cols):
    group = peers // 2
    return (
        pl.BlockSpec((group * cols, COL_WIDTH), lambda j: (j, ROW_WIDTH // COL_WIDTH)),
        pl.BlockSpec((group, 3, cols, COL_WIDTH), lambda j: (j, 0, 0, 0)),
    )


def pack(queries, keys, values, peers):
    cols = queries.shape[0] // peers
    apart, together = pack_specs(peers, cols)
    return pl.pallas_call(
        pack_kernel,
        grid=(2,),
        in_specs=[apart] * 3,
        out_specs=together,
        out_shape=jax.ShapeDtypeStruct((peers, 3, cols, COL_WIDTH), BF16),
        compiler_params=params(),
        cost_estimate=cost("pack"),
        name="pack",
    )(queries, keys, values)


def unpack_kernel(in_ref, _q, _k, _v, dq_ref, dk_ref, dv_ref):
    group = in_ref.shape[0] // pl.num_programs(0)
    peers = pl.ds(pl.program_id(0) * group, group)
    for n, ref in enumerate((dq_ref, dk_ref, dv_ref)):
        ref[...] = in_ref[peers, n].reshape(ref.shape)


def unpack(packed, dq, dk, dv):
    peers, _, cols, _ = packed.shape
    apart, _ = pack_specs(peers, cols)
    anywhere = pl.BlockSpec(memory_space=pl.ANY)
    return pl.pallas_call(
        unpack_kernel,
        grid=(2,),
        in_specs=[RESIDENT] + [anywhere] * 3,
        out_specs=[apart] * 3,
        out_shape=[jax.ShapeDtypeStruct(dq.shape, BF16)] * 3,
        input_output_aliases={1: 0, 2: 1, 3: 2},
        compiler_params=params(),
        cost_estimate=cost("unpack"),
        name="unpack",
    )(resident(packed), dq, dk, dv)


def column_mask(rows, cols):
    key = lax.broadcasted_iota(jnp.int32, (rows * cols, rows * cols), 0)
    query = lax.broadcasted_iota(jnp.int32, (rows * cols, rows * cols), 1)
    return (key <= query) & (key % cols == query % cols)


def head_tokens(ref, n, unit):
    cols, span = unit
    block = ref[:, cols, span] if n is None else ref[:, n, cols, span]
    return block.reshape(-1, DH)


def column_units(rows, width, span):
    together = max(1, 8 * 128**2 // (rows * span) ** 2)
    units = [
        (slice(c * span, (c + 1) * span), head_span(h))
        for c in range(width // span)
        for h in range(COL_HEADS)
    ]
    return [units[n : n + together] for n in range(0, len(units), together)]


def placed(units, width, span):
    base = pl.program_id(0) * width
    return [
        (pl.ds(pl.multiple_of(base + cols.start, span), span), lanes) for cols, lanes in units
    ]


def column_scores(in_ref, units, mask):
    return [
        [jnp.where(mask, dot(head_tokens(in_ref, 1, unit), head_tokens(in_ref, 0, unit), 1, 1), LOW)]
        for unit in units
    ]


def column_forward_kernel(in_ref, out_ref):
    rows, width, _ = out_ref.shape
    span = min(COLUMN_SPAN, width)
    mask = column_mask(rows, span)
    for units in column_units(rows, width, span):
        sources = placed(units, width, span)
        scores = column_scores(in_ref, sources, mask)
        results = forward_units(scores, [head_tokens(in_ref, 2, unit) for unit in sources])
        for (cols, lanes), result in zip(units, results):
            out_ref[:, cols, lanes] = result.reshape(rows, span, DH)


def column_backward_kernel(in_ref, u_ref, out_ref):
    rows, _, width, _ = out_ref.shape
    span = min(COLUMN_SPAN, width)
    mask = column_mask(rows, span)
    for units in column_units(rows, width, span):
        sources = placed(units, width, span)
        queries, keys, values = [
            [head_tokens(in_ref, n, unit) for unit in sources] for n in range(3)
        ]
        upstreams = [head_tokens(u_ref, None, unit) for unit in sources]
        scores = column_scores(in_ref, sources, mask)
        share_grads = [[dot(v, u, 1, 1)] for v, u in zip(values, upstreams)]
        grads = backward_units(scores, share_grads, queries, keys, upstreams)
        for (cols, lanes), query_grad, key_grad, value_grad in zip(units, *grads):
            for n, grad in enumerate((query_grad, key_grad * FACTOR, value_grad)):
                out_ref[:, n, cols, lanes] = grad.astype(BF16).reshape(rows, span, DH)


def column_call(kernel, packed, upstream, name):
    rows, _, cols, width = packed.shape
    forward = upstream is None
    shape = (rows, cols, width) if forward else (rows, 3, cols, width)
    block = max(min(COLUMN_SPAN, cols), cols // 2)
    if forward:
        out_spec = pl.BlockSpec((rows, block, width), lambda c: (0, c, 0))
    else:
        out_spec = pl.BlockSpec((rows, 3, block, width), lambda c: (0, 0, c, 0))
    operands = (packed,) if forward else (packed, upstream)
    return pl.pallas_call(
        kernel,
        grid=(cols // block,),
        in_specs=[RESIDENT] * len(operands),
        out_specs=out_spec,
        out_shape=COLUMN_OUT(shape, BF16),
        compiler_params=params(),
        cost_estimate=cost(name),
        name=name,
    )(*map(resident, operands))


def upstream_kernel(place_ref, *refs):
    *w_refs, cot_ref, up_ref, full_ref = refs
    each, rows, _ = w_refs[0].shape

    @pl.when(pl.program_id(0) == 0)
    def _():
        for n, w_ref in enumerate(w_refs):
            for m in range(each):
                at = pl.multiple_of(place_ref[n * each + m], rows)
                full_ref[pl.ds(at, rows), :] = w_ref[m]

    up_ref[...] = dot(cot_ref[...], full_ref[...], 1, 1).astype(BF16)


def upstream_of(place, pieces, cotangent, name):
    steps, model = cotangent.shape
    each, rows, _ = pieces[0].shape
    width = each * len(pieces) * rows
    block = min(2 * BLOCK, steps)
    return pl.pallas_call(
        upstream_kernel,
        grid=(steps // block,),
        in_specs=[
            pl.BlockSpec(memory_space=pltpu.SMEM),
            *[whole(piece.shape) for piece in pieces],
            pl.BlockSpec((block, model), lambda t: (t, 0)),
        ],
        out_specs=[pl.BlockSpec((block, width), lambda t: (t, 0)), whole((width, model))],
        out_shape=[
            jax.ShapeDtypeStruct((steps, width), BF16),
            jax.ShapeDtypeStruct((width, model), BF16),
        ],
        compiler_params=params(),
        cost_estimate=cost(name),
        name=name,
    )(place, *pieces, cotangent)


def layer_kernel(row_ref, col_ref, w_row_ref, w_col_ref, out_ref):
    out_ref[...] = (
        dot(row_ref[...], w_row_ref[...], 1, 0) + dot(col_ref[...], w_col_ref[...], 1, 0)
    ).astype(BF16)


def layer_output(attn_row, attn_col, w_row, w_col):
    steps, width = attn_row.shape
    model = w_row.shape[1]
    block = min(BLOCK, steps)
    return pl.pallas_call(
        layer_kernel,
        grid=(steps // block,),
        in_specs=[pl.BlockSpec((block, width), lambda t: (t, 0))] * 2 + [whole(w_row.shape)] * 2,
        out_specs=pl.BlockSpec((block, model), lambda t: (t, 0)),
        out_shape=jax.ShapeDtypeStruct((steps, model), BF16),
        compiler_params=params(),
        cost_estimate=cost("layer_output"),
        name="layer_output",
    )(attn_row, attn_col, w_row, w_col)


def weight_kernel(factor, core_ref, attn_ref, cot_ref, keep_ref, send_ref):
    depths, pairs, rows, _ = keep_ref.shape
    product = dot(attn_ref[...], cot_ref[...], 0, 0) * factor
    first = core_ref[0] == 0
    for n in range(pairs):
        for z in range(depths):
            even, odd = [
                product[head * DH + z * rows : head * DH + (z + 1) * rows]
                for head in (2 * n, 2 * n + 1)
            ]
            keep_ref[z, n] = jnp.where(first, even, odd)
            send_ref[z, n] = jnp.where(first, odd, even).astype(send_ref.dtype)


def weight_parts(core, attn, cotangent, factor, depths, dtype, name):
    steps, width = attn.shape
    model = cotangent.shape[1]
    block = min(512, model)
    shape = (depths, width // DH // 2, DH // depths, model)
    out = pl.BlockSpec(shape[:-1] + (block,), lambda n: (0, 0, 0, n))
    return pl.pallas_call(
        functools.partial(weight_kernel, factor),
        grid=(model // block,),
        in_specs=[
            pl.BlockSpec(memory_space=pltpu.SMEM),
            whole((steps, width)),
            pl.BlockSpec((steps, block), lambda n: (0, n)),
        ],
        out_specs=[out, out],
        out_shape=[jax.ShapeDtypeStruct(shape, F32), jax.ShapeDtypeStruct(shape, dtype)],
        compiler_params=params(),
        cost_estimate=cost(name),
        name=name,
    )(core, attn, cotangent)


def flip(array, axis, bits, size):
    return lax.ppermute(array, axis, [(n, n ^ bits) for n in range(size)])


def after(member, *others):
    return lax.optimization_barrier((member, *others))[0]


def over_dp(pieces, dp_size):
    return [flip(piece, "dp", e, dp_size) for e, piece in enumerate(pieces, 1)]


def over_core(member, seq_size):
    return flip(member, "seq", 1, seq_size)


def over_plane(pieces, seq_size):
    return [flip(piece, "seq", 2 * d, seq_size) for d, piece in enumerate(pieces, 1)]


def gather_plane(shard, seq_size):
    pairs = seq_size // 2
    near = [shard, *over_plane([shard] * (pairs - 1), seq_size)]
    close, far = jnp.stack(near[: pairs // 2]), jnp.stack(near[pairs // 2 :])
    upper = lax.axis_index("seq") // 2 >= pairs // 2
    return jnp.where(upper, close, far), jnp.where(upper, far, close)


def piece_places(rows, seq_size, dp_size):
    me = lax.axis_index("seq")
    half = seq_size // 4
    c = (jnp.arange(2) ^ (me % 2))[:, None, None]
    z = (jnp.arange(dp_size) ^ lax.axis_index("dp"))[None, :, None]
    pair = (jnp.arange(half) ^ (me // 2 % half))[None, None, :]
    return (((pair * 2 + c) * dp_size + z) * rows).reshape(-1).astype(jnp.int32)


def cut_up(addends, me):
    def part(n):
        return functools.reduce(
            jnp.add,
            [lax.dynamic_index_in_dim(a, me ^ n, 0, False).astype(F32) for a in addends],
        )

    return part(0), [part(n).astype(BF16) for n in range(1, addends[0].shape[0])]


def sum_up(own, arrived):
    return functools.reduce(jnp.add, [member.astype(F32) for member in arrived], own)


def plane_kernel(pair_ref, *refs):
    *in_refs, own_ref, out_ref, total_ref = refs
    half, others = len(in_refs) // 2, out_ref.shape[0]
    for n in range(2):
        own, *arrived = in_refs[n * half : (n + 1) * half]
        rows = slice(n * own.shape[0], (n + 1) * own.shape[0])
        total_ref[rows] = sum_up(own[...], [ref[...] for ref in arrived])
    own_ref[...] = total_ref[pair_ref[0]]
    for d in range(others):
        out_ref[d] = total_ref[pair_ref[0] ^ (d + 1)].astype(BF16)


def plane_pieces(pair, row_own, row_sent, col_own, col_sent):
    operands = [row_own, *row_sent, col_own, *col_sent]
    pairs, rows, model = row_own.shape
    own, out = pl.pallas_call(
        plane_kernel,
        in_specs=[pl.BlockSpec(memory_space=pltpu.SMEM)] + [RESIDENT] * len(operands),
        out_specs=[RESIDENT] * 2,
        out_shape=[
            pltpu.VMEM((rows, model), F32),
            pltpu.VMEM((2 * pairs - 1, rows, model), BF16),
        ],
        scratch_shapes=[pltpu.VMEM((2 * pairs, rows, model), F32)],
        compiler_params=params(),
        cost_estimate=cost("plane_pieces"),
        name="plane_pieces",
    )(pair.reshape(1).astype(jnp.int32), *map(resident, operands))
    return own, [out[d] for d in range(out.shape[0])]


def body(queries, keys, values, out_weight, cotangent):
    seq_size, dp_size = lax.axis_size("seq"), lax.axis_size("dp")
    shape, cot_shape = queries.shape, cotangent.shape
    queries, keys, values, cotangent = [
        member.reshape(-1, member.shape[-1]) for member in (queries, keys, values, cotangent)
    ]
    steps = queries.shape[0]
    model = cotangent.shape[1]
    rows = out_weight.shape[0]
    factor = 1.0 / math.sqrt(steps * seq_size * dp_size)
    core = (lax.axis_index("seq") % 2).reshape(1).astype(jnp.int32)
    staged = seq_size == ROW_HEADS + COL_HEADS and rows % 16 == 0

    def exchange(member):
        return lax.all_to_all(member, "seq", split_axis=0, concat_axis=0, tiled=True)

    def weights(attn, name):
        return weight_parts(core, attn, cotangent, factor, dp_size, BF16, name)

    packed = pack(queries, keys, values, seq_size)
    arrived = exchange(packed)
    if staged:
        pair, depth = lax.axis_index("seq") // 2, lax.axis_index("dp")
        place = piece_places(rows, seq_size, dp_size)
        col_mine, row_mine = gather_plane(out_weight, seq_size)
        col_depth = [col_mine, *over_dp([col_mine] * (dp_size - 1), dp_size)]
        attn_row = row_forward(queries, keys, values, packed, col_mine)
        row_keep, row_send = weights(attn_row, "weight_row")
        col_depth = [after(member, row_keep) for member in col_depth]
        col_pieces = col_depth + [over_core(member, seq_size) for member in col_depth]
        row_received = over_core(after(row_send, *col_pieces), seq_size)
        row_mine = after(row_mine, *col_depth)
        row_depth = [row_mine, *over_dp([row_mine] * (dp_size - 1), dp_size)]
        arrived = after(arrived, row_keep)
        then = [row_depth[1]]
    else:
        place = jnp.zeros((1,), jnp.int32)
        full = lax.all_gather(out_weight, ("seq", "dp"), axis=0, tiled=True)
        row_pieces, col_pieces = [full[None, :ROW_WIDTH]], [full[None, ROW_WIDTH:]]
        attn_row = row_forward(queries, keys, values)
        then = []

    out_col = column_call(column_forward_kernel, arrived, None, "column_forward")
    attn_col = exchange(out_col).reshape(steps, COL_WIDTH)
    up_col, w_col = upstream_of(
        place, col_pieces, after(cotangent, out_col, *then), "upstream_col"
    )
    then = []
    if staged:
        row_own, row_out = cut_up((row_keep, after(row_received, up_col)), depth)
        row_pieces = row_depth + [
            over_core(after(member, up_col), seq_size) for member in row_depth
        ]
        then = row_depth + row_out
    up_arrived = exchange(after(up_col, attn_col, *then).reshape(seq_size, -1, COL_WIDTH))
    then = []
    if staged:
        row_sent = over_dp([after(piece, *row_depth) for piece in row_out], dp_size)
        col_keep, col_send = weights(attn_col, "weight_col")
        col_received = over_core(col_send, seq_size)
        then = [col_keep, *row_pieces, *row_sent[:SENT_FIRST]]
    up_arrived = after(up_arrived, *then)
    grads_col = column_call(column_backward_kernel, arrived, up_arrived, "column_backward")
    if staged:
        grads_col = after(grads_col, col_received)
    grads_arrived = exchange(grads_col)
    then = [grads_col]
    if staged:
        col_own, col_out = cut_up((after(col_keep, grads_col), col_received), depth)
        col_sent = over_dp(col_out, dp_size)
        then = col_out
    up_row, w_row = upstream_of(place, row_pieces, after(cotangent, *then), "upstream_row")
    dq, dk, dv = row_backward(queries, keys, values, up_row)
    layer_out = layer_output(after(attn_row, dq), attn_col, w_row, w_col)
    if staged:
        own, out = plane_pieces(
            pair,
            row_own,
            row_sent,
            col_own,
            [after(member, layer_out) for member in col_sent],
        )
        sent = over_plane(out, seq_size)
        dq, dk, dv = unpack(after(grads_arrived, *out), dq, dk, dv)
        weight_grad = sum_up(own, [after(member, dq) for member in sent])
    else:
        local = []
        for member, name in ((attn_row, "weight_row"), (attn_col, "weight_col")):
            even, odd = weight_parts(
                jnp.zeros((1,), jnp.int32), member, cotangent, factor, 1, F32, name
            )
            local.append(jnp.stack([even[0], odd[0]], axis=1).reshape(-1, model))
        weight_grad = lax.psum_scatter(
            jnp.concatenate(local), ("seq", "dp"), scatter_dimension=0, tiled=True
        )
        dq, dk, dv = unpack(grads_arrived, dq, dk, dv)
    return (
        layer_out.reshape(cot_shape),
        dq.reshape(shape),
        dk.reshape(shape),
        dv.reshape(shape),
        weight_grad,
    )


def solution(mesh):
    tokens = P("dp", "seq", None, None)
    weights = P(("seq", "dp"), None)
    return jax.shard_map(
        body,
        mesh=mesh,
        in_specs=(tokens, tokens, tokens, weights, tokens),
        out_specs=(tokens, tokens, tokens, tokens, weights),
        check_vma=False,
    )
```
